128 devices in a mesh: by: 8 (over x, core), bx: 16 (over y, z).
Axes of the slice: x: 4, y: 4, z: 4, core: 2. Of those that a mesh axis runs over, the one named last changes fastest.
Arguments:
- tracer_one: float32 [18, 512, 4096], P(None, 'by', 'bx'), may hold values from -6 to 6
- tracer_two: float32 [18, 512, 4096], P(None, 'by', 'bx'), may hold values from -6 to 6
- east_flow: bfloat16 [18, 512, 4096], P(None, 'by', 'bx'), may hold values from -0.3984375 to 0.3984375
- north_flow: bfloat16 [18, 512, 4096], P(None, 'by', 'bx'), may hold values from -0.3984375 to 0.3984375
- depth_levels: int32 [512, 4096], P('by', 'bx'), may hold values from 0 to 18
- side_mix: float32 [18], replicated, may hold values from 0.02 to 0.2
- vert_mix: float32 [18], replicated, may hold values from 0.01 to 0.3
- thickness: float32 [18], replicated, may hold values from 0.1 to 0.4
- corner_depth: float32 [512, 4096], P('by', 'bx'), may hold values from 0.5 to 4
- diagonal: float32 [512, 4096], P('by', 'bx'), may hold values from 0.05 to 0.5
Outputs:
- new_one: float32 [18, 512, 4096], P(None, 'by', 'bx')
- new_two: float32 [18, 512, 4096], P(None, 'by', 'bx')
- surface: float32 [512, 4096], P('by', 'bx')
The draws below stay inside these ranges and needn't reach their ends.
All inputs are finite; a program needn't handle non-finite values.
Results may differ from the reference program's by a relative error of at most 0.0003.
Values may be sent and summed in bfloat16 or wider, within the bound.
No kernel may reach another device: no remote copies, remote signals or barrier semaphores. Data moves between devices by JAX's collectives and lax.ppermute only.
A program may use at most 192 MiB of HBM per device.

```python
import math
import jax
import jax.numpy as jnp
from jax import lax

LEV = 18
ITERS = 3
NX = 4096
NY = 512


def touch_ends(result, stream_key, least, top_value):
    longest = result.shape.index(max(result.shape))
    spots = []
    for shift in (0, 1):
        where = [jax.random.randint(jax.random.fold_in(stream_key, axis), (), 0, length) for axis, length in enumerate(result.shape)]
        where[longest] = (where[longest] + shift) % result.shape[longest]
        spots.append(tuple(where))
    return result.at[spots[0]].set(least).at[spots[1]].set(top_value)


def shard_levels(own_key, dims, pieces, smallest, high):
    factor_of = 1.0
    for position, parts in pieces:
        heights = jax.random.uniform(jax.random.fold_in(jax.random.fold_in(own_key, 6), position), (parts,), jnp.float32, smallest / len(pieces), high / len(pieces))
        factor_of = factor_of * jnp.repeat(jnp.exp(heights), dims[position] // parts).reshape((-1,) + (1,) * (len(dims) - 1 - position))
    return factor_of


def gaussian(key, extent, deviation, bound, pieces=(), kind=jnp.bfloat16):
    drawn = deviation * jax.random.normal(key, extent, jnp.float32)
    if pieces:
        drawn = drawn * shard_levels(key, extent, pieces, -0.22, 0.18)
    return jnp.clip(drawn, -bound, bound).astype(kind)


def setup_inputs(seed: int = 0) -> dict:
    keys = jax.random.split(jax.random.key(seed), 11)
    return {
        "tracer_one": gaussian(keys[0], (LEV, NY, NX), 1.0, 6.0, ((1, 8), (2, 16)), jnp.float32),
        "tracer_two": gaussian(keys[1], (LEV, NY, NX), 1.0, 6.0, ((1, 8), (2, 16)), jnp.float32),
        "east_flow": jnp.clip(jax.random.uniform(keys[2], (LEV, NY, NX), jnp.float32, -0.3984375, 0.3984375) * shard_levels(keys[2], (LEV, NY, NX), ((1, 8), (2, 16)), -0.4, 0.0), -0.3984375, 0.3984375).astype(jnp.bfloat16),
        "north_flow": jnp.clip(jax.random.uniform(keys[3], (LEV, NY, NX), jnp.float32, -0.3984375, 0.3984375) * shard_levels(keys[3], (LEV, NY, NX), ((1, 8), (2, 16)), -0.4, 0.0), -0.3984375, 0.3984375).astype(jnp.bfloat16),
        "depth_levels": touch_ends(jax.random.randint(keys[4], (NY, NX), 0, LEV + 1), jax.random.fold_in(keys[4], 1), 0, LEV).astype(jnp.int32),
        "side_mix": jnp.clip(jnp.exp(jax.random.uniform(keys[5], (LEV,), jnp.float32, math.log(0.02), math.log(0.2))), 0.02, 0.2),
        "vert_mix": jnp.clip(jnp.exp(jax.random.uniform(keys[6], (LEV,), jnp.float32, math.log(0.01), math.log(0.3))), 0.01, 0.3),
        "thickness": jnp.clip(jnp.exp(jax.random.uniform(keys[7], (LEV,), jnp.float32, math.log(0.1), math.log(0.4))), 0.1, 0.4),
        "corner_depth": jnp.clip(jnp.exp(math.log(4.0) - 2.0794415 * jax.random.uniform(keys[8], (NY, NX), jnp.float32) ** shard_levels(keys[8], (NY, NX), ((0, 8), (1, 16)), -0.2, 0.2)), 0.5, 4.0),
        "diagonal": jnp.clip(jnp.exp(math.log(0.5) - 2.3025851 * jax.random.uniform(keys[9], (NY, NX), jnp.float32) ** shard_levels(keys[9], (NY, NX), ((0, 8), (1, 16)), -0.2, 0.2)), 0.05, 0.5),
    }


def pad_field(field):
    field = jnp.pad(field, [(0, 0)] * (field.ndim - 1) + [(1, 1)], mode="wrap")
    return jnp.pad(field, [(0, 0)] * (field.ndim - 2) + [(1, 1), (0, 0)])


def horizontal(padded, side):
    tracers = padded[0:2]
    east_vel = padded[2]
    north_vel = padded[3]
    wet_pad = padded[4]
    left = tracers[..., 1:-1, :-1]
    right = tracers[..., 1:-1, 1:]
    face_east = wet_pad[..., 1:-1, :-1] * wet_pad[..., 1:-1, 1:]
    east = (east_vel[..., 1:-1, :-1] * 0.5 * (left + right) - side * (right - left)) * face_east
    lower = tracers[..., :-1, 1:-1]
    upper = tracers[..., 1:, 1:-1]
    face_north = wet_pad[..., :-1, 1:-1] * wet_pad[..., 1:, 1:-1]
    north = (north_vel[..., :-1, 1:-1] * 0.5 * (lower + upper) - side * (upper - lower)) * face_north
    return -(east[..., 1:] - east[..., :-1]) - (north[..., 1:, :] - north[..., :-1, :])


def vertical(tracers, wet, vert_mix):
    falling = vert_mix[:-1, None, None] * (tracers[:, 1:] - tracers[:, :-1]) * wet[1:]
    zeros = jnp.zeros_like(tracers[:, :1])
    padded = jnp.concatenate([zeros, falling, zeros], axis=1)
    return padded[:, 1:] - padded[:, :-1]


def corner_operator(extended, depth_ext, field, diagonal):
    cell_a = extended[:-1, :-1]
    cell_b = extended[:-1, 1:]
    cell_c = extended[1:, :-1]
    cell_d = extended[1:, 1:]
    grad_x = 0.5 * ((cell_b + cell_d) - (cell_a + cell_c))
    grad_y = 0.5 * ((cell_c + cell_d) - (cell_a + cell_b))
    flux_x = depth_ext * grad_x
    flux_y = depth_ext * grad_y
    plus = flux_x + flux_y
    minus = flux_x - flux_y
    return (diagonal * field - 0.5 * plus[1:, 1:] + 0.5 * minus[1:, :-1]
            - 0.5 * minus[:-1, 1:] + 0.5 * plus[:-1, :-1])


def chron_gear(forcing, operate, totals):
    surface = jnp.zeros_like(forcing)
    residual = forcing
    image = operate(residual)
    norm_now, product = totals(residual * residual, residual * image)
    alpha = norm_now / product
    direction, along = residual, image
    for step in range(ITERS):
        surface = surface + alpha * direction
        residual = residual - alpha * along
        if step + 1 < ITERS:
            image = operate(residual)
            norm_next, product = totals(residual * residual, residual * image)
            ratio = norm_next / norm_now
            alpha = norm_next / (product - ratio * norm_next / alpha)
            direction = residual + ratio * direction
            along = image + ratio * along
            norm_now = norm_next
    return surface


def global_totals(first, second):
    return jnp.sum(first), jnp.sum(second)


def reference(tracer_one, tracer_two, east_flow, north_flow, depth_levels, side_mix, vert_mix, thickness, corner_depth, diagonal):
    levels = lax.broadcasted_iota(jnp.int32, tracer_one.shape, 0)
    wet = (levels < depth_levels[None]).astype(jnp.float32)

    def level_step(items):
        first, second, east, north, wet_level, side = items
        stacked = jnp.stack([first, second, east.astype(jnp.float32), north.astype(jnp.float32), wet_level])
        return horizontal(pad_field(stacked), side)

    change = lax.map(level_step, (tracer_one, tracer_two, east_flow, north_flow, wet, side_mix))
    change = jnp.transpose(change, (1, 0, 2, 3))
    tracers = jnp.stack([tracer_one, tracer_two])
    updated = wet * (tracers + change + vertical(tracers, wet, vert_mix))
    forcing = jnp.sum(thickness[:, None, None] * (updated[0] - 0.5 * updated[1]), axis=0)
    depth = corner_depth * (depth_levels > 0).astype(jnp.float32)
    depth_ext = pad_field(depth)[:-1, :-1]

    def operate(field):
        return corner_operator(pad_field(field), depth_ext, field, diagonal)

    surface = chron_gear(forcing, operate, global_totals)
    return updated[0], updated[1], surface
```

```python
import jax
import jax.numpy as jnp
from jax import lax
from jax.experimental import pallas as pl
from jax.experimental.pallas import tpu as pltpu
from jax.sharding import PartitionSpec as P

LEV = 18
GROUP = 3
SLOT = 24
ROWS, COLS = 64, 256
WIDE = COLS + 128
TALL = ROWS + 16
F32 = jnp.float32
VMEM = pl.BlockSpec(memory_space=pltpu.VMEM)
SMEM = pl.BlockSpec(memory_space=pltpu.SMEM)
HBM = pl.BlockSpec(memory_space=pl.ANY)
PARAMS = pltpu.CompilerParams(vmem_limit_bytes=48 * 1024 * 1024)


def iota(shape, axis):
    return lax.broadcasted_iota(jnp.int32, shape, axis)


def shape(*dims):
    return jax.ShapeDtypeStruct(dims, F32)


def pairs(size, odd, wrap):
    swaps = []
    for low in range(1 if odd else 0, size, 2):
        high = low + 1
        if high == size and not wrap:
            continue
        swaps += [(low, high % size), (high % size, low)]
    return swaps


def swap_both(first, second, axis, size, wrap):
    return (
        lax.ppermute(first, axis, pairs(size, False, wrap)),
        lax.ppermute(second, axis, pairs(size, True, wrap)),
    )


def by_side(axis, first, second):
    even = lax.axis_index(axis) % 2 == 0
    return jnp.where(even, first, second), jnp.where(even, second, first)


def load_groups(sources, targets, sems):
    def copy(array, group):
        part = pl.ds(group * GROUP, GROUP)
        return pltpu.make_async_copy(sources[array].at[part], targets[array].at[part], sems.at[array, group])

    return copy


def forcing_kernel(side, vert, thick, one_hbm, two_hbm, east_hbm, north_hbm, levels, corner, diag,
                   first_out, second_out, forcing_out, edge_rows,
                   one, two, east, north, east_sum, north_sum, column, right, left, sems):
    copy = load_groups((one_hbm, two_hbm, east_hbm, north_hbm), (one, two, east, north), sems)
    groups = LEV // GROUP
    for group in range(groups):
        for array in range(4):
            copy(array, group).start()
    deep = levels[...]
    at_row, at_col = iota((ROWS, COLS), 0), iota((ROWS, COLS), 1)
    lane = iota((ROWS, 128), 1)
    east_deep = jnp.where(at_col < COLS - 1, jnp.minimum(deep, pltpu.roll(deep, COLS - 1, 1)), 0)
    north_deep = jnp.where(at_row < ROWS - 1, jnp.minimum(deep, pltpu.roll(deep, ROWS - 1, 0)), 0)
    for total in (east_sum, north_sum, column, right, left, edge_rows):
        total[...] = jnp.zeros(total.shape, F32)

    def level(k):
        c_one, c_two = one[k], two[k]
        flow_e, flow_n = east[k].astype(F32), north[k].astype(F32)
        both = c_one - 0.5 * c_two
        weight, mix = thick[k], side[k]
        below, above = jnp.minimum(k + 1, LEV - 1), jnp.maximum(k - 1, 0)
        fall = (weight - thick[below]) * vert[k]
        fall_above = (thick[above] - weight) * vert[above]
        column[...] += both * jnp.where(
            deep > k + 1, weight + fall_above - fall, jnp.where(deep > k, weight + fall_above, 0.0))
        nxt = pltpu.roll(both, COLS - 1, 1)
        east_sum[...] += jnp.where(
            east_deep > k, (0.5 * weight) * (flow_e * (both + nxt)) - (weight * mix) * (nxt - both), 0.0)
        nxt = pltpu.roll(both, ROWS - 1, 0)
        north_sum[...] += jnp.where(
            north_deep > k, (0.5 * weight) * (flow_n * (both + nxt)) - (weight * mix) * (nxt - both), 0.0)
        packed = right[...]
        packed = jnp.where(lane == k, c_one[:, COLS - 1:], packed)
        packed = jnp.where(lane == k + LEV, c_two[:, COLS - 1:], packed)
        packed = jnp.where((lane == k + 2 * LEV) | (lane == k + 3 * LEV), flow_e[:, COLS - 1:], packed)
        right[...] = packed
        packed = left[...]
        packed = jnp.where(lane == k + 64, c_one[:, :1], packed)
        packed = jnp.where(lane == k + 64 + LEV, c_two[:, :1], packed)
        left[...] = packed
        edge_rows[pl.ds(k, 1), :] = c_one[:1]
        edge_rows[pl.ds(SLOT + k, 1), :] = c_two[:1]
        edge_rows[pl.ds(2 * SLOT + k, 1), :] = c_one[ROWS - 1:]
        edge_rows[pl.ds(3 * SLOT + k, 1), :] = c_two[ROWS - 1:]
        edge_rows[pl.ds(4 * SLOT + k, 1), :] = flow_n[ROWS - 1:]

    @pl.loop(0, groups)
    def _(group):
        for array in range(4):
            copy(array, group).wait()
        for step in range(GROUP):
            level(group * GROUP + step)

    e_sum, n_sum = east_sum[...], north_sum[...]
    forcing = column[...] - (e_sum - pltpu.roll(e_sum, 1, 1)) - (n_sum - pltpu.roll(n_sum, 1, 0))
    forcing_out[...] = forcing
    depth = jnp.where(deep > 0, corner[...], 0.0)
    fields = (forcing, depth, diag[...], deep.astype(F32))
    to_right, to_left = right[...], left[...]
    for i, field in enumerate(fields):
        tile = field[:, COLS - 128:]
        tile = pltpu.roll(tile, 128 - 2 * i, 1) if i else tile
        to_right = jnp.where((lane >= 126 - 2 * i) & (lane < 128 - 2 * i), tile, to_right)
        tile = field[:, :128]
        tile = pltpu.roll(tile, 3 * i, 1) if i else tile
        to_left = jnp.where((lane >= 3 * i) & (lane < 3 * i + 3), tile, to_left)
    rows_0 = edge_rows[0:SLOT] - 0.5 * edge_rows[SLOT:2 * SLOT]
    rows_1 = edge_rows[2 * SLOT:3 * SLOT] - 0.5 * edge_rows[3 * SLOT:4 * SLOT]
    rows_2 = edge_rows[4 * SLOT:5 * SLOT]
    lane = iota((SLOT, 128), 1)
    corner_right = corner_left = jnp.zeros((SLOT, 128), F32)
    for i, rows in enumerate((rows_0, rows_1, rows_2)):
        tile = rows[:, COLS - 128:]
        tile = pltpu.roll(tile, 128 - 2 * i, 1) if i else tile
        corner_right = jnp.where((lane >= 126 - 2 * i) & (lane < 128 - 2 * i), tile, corner_right)
        tile = rows[:, :128]
        tile = pltpu.roll(tile, 3 * i, 1) if i else tile
        corner_left = jnp.where((lane >= 3 * i) & (lane < 3 * i + 3), tile, corner_left)
    even = lax.axis_index("bx") % 2 == 0
    first_out[:ROWS] = jnp.where(even, to_right, to_left)
    second_out[:ROWS] = jnp.where(even, to_left, to_right)
    first_out[ROWS:] = jnp.where(even, corner_right, corner_left)
    second_out[ROWS:] = jnp.where(even, corner_left, corner_right)


def lane_tile(from_right, from_left, i):
    lane = iota(from_right.shape, 1)
    if i:
        from_right, from_left = pltpu.roll(from_right, 128 - 3 * i, 1), pltpu.roll(from_left, 2 * i, 1)
    return jnp.where(lane < 3, from_right, jnp.where(lane >= 126, from_left, 0.0))


def columns_kernel(side, thick, first, second, first_in, second_in, forcing, levels, corner, diag, edge_rows,
                   first_out, second_out, forcing_wide, depth_wide, diag_wide, flux_left, flux_right):
    own_right, own_left = by_side("bx", first[...], second[...])
    from_right, from_left = by_side("bx", first_in[...], second_in[...])
    deep = levels[...]
    deep_f = deep.astype(F32)
    lane = iota((ROWS, 128), 1)
    at = iota((8, 128), 1)
    mix, weight = jnp.zeros((8, 128), F32), jnp.zeros((8, 128), F32)
    for k in range(LEV):
        mix = jnp.where((at == k) | (at == k + LEV), side[k], mix)
        weight = jnp.where(at == k, thick[k], jnp.where(at == k + LEV, -0.5 * thick[k], weight))
    mix, weight = mix[:1], weight[:1]
    of_lane = jnp.where(at < LEV, at, jnp.where(at < 2 * LEV, at - LEV, 100))[:1].astype(F32)

    def face(west, east, flow, west_deep, east_deep):
        flux = 0.5 * flow * (west + east) - mix * (east - west)
        flux = jnp.where(of_lane < jnp.minimum(west_deep, east_deep), flux, 0.0)
        return flux, jnp.sum(flux * weight, axis=1, keepdims=True)

    own, seen = own_left[:ROWS], from_left[:ROWS]
    flux, west_sum = face(seen, pltpu.roll(own, 64, 1), pltpu.roll(seen, 128 - 2 * LEV, 1), seen[:, 121:122], deep_f[:, :1])
    flux_left[...] = flux
    own, seen = own_right[:ROWS], from_right[:ROWS]
    flux, east_sum = face(own, pltpu.roll(seen, 64, 1), pltpu.roll(own, 128 - 2 * LEV, 1), deep_f[:, COLS - 1:], seen[:, 9:10])
    flux_right[...] = flux

    mine = forcing[...]
    tiles = (
        mine[:, :128] + jnp.where(lane == 0, west_sum, 0.0),
        mine[:, 128:] - jnp.where(lane == 127, east_sum, 0.0),
        lane_tile(from_right[:ROWS], from_left[:ROWS], 0)
        + jnp.where(lane == 0, east_sum, jnp.where(lane == 127, -west_sum, 0.0)),
    )
    wide = jnp.concatenate(tiles, axis=1)
    forcing_wide[...] = wide
    depth = jnp.where(deep > 0, corner[...], 0.0)
    depth_w = jnp.concatenate([depth, lane_tile(from_right[:ROWS], from_left[:ROWS], 1)], axis=1)
    diag_w = jnp.concatenate([diag[...], lane_tile(from_right[:ROWS], from_left[:ROWS], 2)], axis=1)
    deep_w = jnp.concatenate([deep_f, lane_tile(from_right[:ROWS], from_left[:ROWS], 3)], axis=1)
    depth_wide[...] = depth_w
    diag_wide[...] = diag_w

    def rows(value, i):
        return jnp.concatenate([value, lane_tile(from_right[ROWS:], from_left[ROWS:], i)], axis=1)

    nothing = jnp.zeros((SLOT, 128), F32)
    two_0, two_1 = edge_rows[SLOT:2 * SLOT], edge_rows[3 * SLOT:4 * SLOT]
    both_0 = rows(edge_rows[0:SLOT] - 0.5 * two_0, 0)
    both_1 = rows(edge_rows[2 * SLOT:3 * SLOT] - 0.5 * two_1, 1)
    north_1 = rows(edge_rows[4 * SLOT:5 * SLOT], 2)
    even = lax.axis_index("by") % 2 == 0
    up = (both_1, jnp.concatenate([two_1, nothing], axis=1), north_1, jnp.concatenate(
        [wide[62:64], deep_w[63:64], depth_w[62:64], diag_w[63:64], jnp.zeros((2, WIDE), F32)], axis=0))
    down = (both_0, jnp.concatenate([two_0, nothing], axis=1), jnp.zeros((SLOT, WIDE), F32), jnp.concatenate(
        [wide[0:3], deep_w[0:1], depth_w[0:2], diag_w[0:2]], axis=0))
    for i in range(4):
        place = slice(i * SLOT, i * SLOT + (SLOT if i < 3 else 8))
        first_out[place] = jnp.where(even, up[i], down[i])
        second_out[place] = jnp.where(even, down[i], up[i])


def operate(field, half_depth, diag):
    east = pltpu.roll(field, WIDE - 1, 1)
    north = pltpu.roll(field, TALL - 1, 0)
    corner = pltpu.roll(north, WIDE - 1, 1)
    plus = half_depth * (corner - field)
    minus = half_depth * (east - north)
    return (diag * field - plus + pltpu.roll(minus, 1, 1)
            + pltpu.roll(pltpu.roll(plus, 1, 1) - minus, 1, 0)), plus, minus


def solver_kernel(side, thick, first, second, first_in, second_in, forcing, depth, diag,
                  zero_out, one_out, two_out, sums_out, flux_rows):
    own_up, own_down = by_side("by", first[...], second[...])
    above, beneath = by_side("by", first_in[...], second_in[...])
    level = iota((SLOT, WIDE), 0)
    mix, weight = jnp.zeros((SLOT, WIDE), F32), jnp.zeros((SLOT, WIDE), F32)
    for k in range(LEV):
        mix = jnp.where(level == k, side[k], mix)
        weight = jnp.where(level == k, thick[k], weight)
    level_f = level.astype(F32)

    def face(south, north, south_deep, north_deep, place):
        flow = south[2 * SLOT:3 * SLOT]
        wet = level_f < jnp.minimum(south_deep, north_deep)

        def flux(low, high):
            columns = low.shape[1]
            value = 0.5 * flow[:, :columns] * (low + high) - mix[:, :columns] * (high - low)
            return jnp.where(wet[:, :columns], value, 0.0)

        both = flux(south[:SLOT], north[:SLOT])
        two = flux(south[SLOT:2 * SLOT, :COLS], north[SLOT:2 * SLOT, :COLS])
        flux_rows[place * SLOT:(place + 1) * SLOT] = both[:, :COLS] + 0.5 * two
        flux_rows[(place + 1) * SLOT:(place + 2) * SLOT] = two
        return jnp.sum(both * weight, axis=0, keepdims=True)

    top = face(own_up, above, own_up[74:75], above[75:76], 0)
    bottom = face(beneath, own_down, beneath[74:75], own_down[75:76], 2)

    def blank(count):
        return jnp.zeros((count, WIDE), F32)

    own_row = iota((ROWS, WIDE), 0)
    mine = forcing[...] + jnp.where(own_row == 0, bottom, jnp.where(own_row == ROWS - 1, -top, 0.0))
    field = jnp.concatenate([
        jnp.concatenate([blank(6), beneath[72:73], beneath[73:74] - bottom], axis=0), mine,
        jnp.concatenate([above[72:73] + top, above[73:75], blank(5)], axis=0)], axis=0)
    half_depth = 0.5 * jnp.concatenate([
        jnp.concatenate([blank(6), beneath[75:77]], axis=0), depth[...],
        jnp.concatenate([above[76:78], blank(6)], axis=0)], axis=0)
    diag_all = jnp.concatenate([
        jnp.concatenate([blank(7), beneath[77:78]], axis=0), diag[...],
        jnp.concatenate([above[78:80], blank(6)], axis=0)], axis=0)
    last = lax.axis_index("by") == lax.axis_size("by") - 1
    inside = iota((TALL, WIDE), 0) < jnp.where(last, ROWS + 8, TALL)

    image, _, _ = operate(field, half_depth, diag_all)
    image = jnp.where(inside, image, 0.0)
    twice, _, _ = operate(image, half_depth, diag_all)
    twice = jnp.where(inside, twice, 0.0)
    _, plus, minus = operate(twice, half_depth, diag_all)
    east = pltpu.roll(twice, WIDE - 1, 1)
    north = pltpu.roll(twice, TALL - 1, 0)
    corner = pltpu.roll(north, WIDE - 1, 1)
    energy = diag_all * twice * twice + plus * (corner - twice) + minus * (east - north)

    def own(value):
        return value[8:8 + ROWS, :COLS]

    v_0, v_1, v_2 = own(field), own(image), own(twice)
    zero_out[...], one_out[...], two_out[...] = v_0, v_1, v_2
    lane = iota((128, 128), 1)
    sums = jnp.zeros((128, 128), F32)
    for i, product in enumerate((v_0 * v_0, v_0 * v_1, v_1 * v_1, v_1 * v_2, v_2 * v_2, own(energy))):
        sums = jnp.where(lane == i, jnp.sum(product, keepdims=True), sums)
    sums_out[...] = sums


def surface_kernel(sums, zero, one, two, surface):
    total = jnp.sum(sums[...], axis=0, keepdims=True)
    m = [total[:, i:i + 1] for i in range(6)]
    a_0 = m[0] / m[1]
    rr_1 = m[0] - 2.0 * a_0 * m[1] + a_0 * a_0 * m[2]
    rar_1 = m[1] - 2.0 * a_0 * m[2] + a_0 * a_0 * m[3]
    b_1 = rr_1 / m[0]
    a_1 = rr_1 / (rar_1 - b_1 * rr_1 / a_0)
    grow = 1.0 + b_1
    p_1 = -(a_0 + a_1 * grow)
    p_2 = a_1 * a_0
    rr_2 = m[0] + p_1 * p_1 * m[2] + p_2 * p_2 * m[4] + 2.0 * (p_1 * m[1] + p_2 * m[2] + p_1 * p_2 * m[3])
    rar_2 = m[1] + p_1 * p_1 * m[3] + p_2 * p_2 * m[5] + 2.0 * (p_1 * m[2] + p_2 * m[3] + p_1 * p_2 * m[4])
    b_2 = rr_2 / rr_1
    a_2 = rr_2 / (rar_2 - b_2 * rr_2 / a_1)
    w_0 = a_0 + a_1 * grow + a_2 * (1.0 + b_2 * grow)
    w_1 = -a_1 * a_0 + a_2 * (p_1 - b_2 * a_0)
    w_2 = a_2 * p_2
    surface[...] = w_0 * zero[...] + w_1 * one[...] + w_2 * two[...]


def tracers_kernel(side, vert, one_hbm, two_hbm, east_hbm, north_hbm, levels, flux_left, flux_right, flux_rows,
                   one_out, two_out, one, two, east, north, new_one, new_two, sems, out_sems):
    copy = load_groups((one_hbm, two_hbm, east_hbm, north_hbm), (one, two, east, north), sems)
    groups = LEV // GROUP
    for group in range(groups):
        for array in range(4):
            copy(array, group).start()

    def store(array, group):
        part = pl.ds(group * GROUP, GROUP)
        source, target = ((new_one, one_out), (new_two, two_out))[array]
        return pltpu.make_async_copy(source.at[part], target.at[part], out_sems.at[array, group])

    deep = levels[...]
    at_row, at_col = iota((ROWS, COLS), 0), iota((ROWS, COLS), 1)
    lane = iota((ROWS, 128), 1)
    east_deep = jnp.minimum(deep, pltpu.roll(deep, COLS - 1, 1))
    north_deep = jnp.minimum(deep, pltpu.roll(deep, ROWS - 1, 0))

    def level(k):
        flow_e, flow_n = 0.5 * east[k].astype(F32), 0.5 * north[k].astype(F32)
        mix = side[k]
        below, above = jnp.minimum(k + 1, LEV - 1), jnp.maximum(k - 1, 0)
        fall_w, fall_above_w = vert[k], vert[above]
        wet, wet_below = deep > k, deep > k + 1
        wet_east, wet_north = east_deep > k, north_deep > k
        for i, (source, target) in enumerate(((one, new_one), (two, new_two))):
            c = source[k]
            nxt = pltpu.roll(c, COLS - 1, 1)
            e = jnp.where(wet_east, flow_e * (c + nxt) - mix * (nxt - c), 0.0)
            seam = pltpu.roll(flux_right[...], 127 - k - i * LEV, 1)
            e = jnp.concatenate([e[:, :128], jnp.where(lane == 127, seam, e[:, 128:])], axis=1)
            e_west = pltpu.roll(e, 1, 1)
            seam = pltpu.roll(flux_left[...], (256 - k - i * LEV) % 128, 1)
            e_west = jnp.concatenate([jnp.where(lane == 0, seam, e_west[:, :128]), e_west[:, 128:]], axis=1)
            nxt = pltpu.roll(c, ROWS - 1, 0)
            n = jnp.where(wet_north, flow_n * (c + nxt) - mix * (nxt - c), 0.0)
            n = jnp.where(at_row == ROWS - 1, flux_rows[pl.ds(i * SLOT + k, 1), :], n)
            n_south = pltpu.roll(n, 1, 0)
            n_south = jnp.where(at_row == 0, flux_rows[pl.ds((2 + i) * SLOT + k, 1), :], n_south)
            fall = jnp.where(wet_below, fall_w * (source[below] - c), 0.0)
            fall_above = fall_above_w * (c - source[above])
            target[k] = jnp.where(wet, c - (e - e_west) - (n - n_south) + (fall - fall_above), 0.0)

    for array in range(4):
        copy(array, 0).wait()

    @pl.loop(0, groups)
    def _(group):
        @pl.when(group + 1 < groups)
        def _():
            for array in range(4):
                copy(array, group + 1).wait()

        for step in range(GROUP):
            level(group * GROUP + step)
        for array in range(2):
            store(array, group).start()

    for group in range(groups):
        for array in range(2):
            store(array, group).wait()


def level_scratch():
    block = (LEV, ROWS, COLS)
    return [pltpu.VMEM(block, F32), pltpu.VMEM(block, F32), pltpu.VMEM(block, jnp.bfloat16), pltpu.VMEM(block, jnp.bfloat16)]


def cost(flops, moved):
    return pl.CostEstimate(flops=flops, bytes_accessed=moved, transcendentals=0)


def on_device(tracer_one, tracer_two, east_flow, north_flow, depth_levels, side_mix, vert_mix, thickness,
              corner_depth, diagonal):
    n_by, n_bx = lax.axis_size("by"), lax.axis_size("bx")
    cells = LEV * ROWS * COLS
    plane = shape(ROWS, COLS)
    wide = shape(ROWS, WIDE)
    column_message, row_message = shape(ROWS + SLOT, 128), shape(3 * SLOT + 8, WIDE)
    flat = pltpu.VMEM((ROWS, COLS), F32)
    tile = pltpu.VMEM((ROWS, 128), F32)
    transfers = pltpu.SemaphoreType.DMA((4, LEV // GROUP))
    first, second, forcing, edge_rows = pl.pallas_call(
        forcing_kernel,
        out_shape=(column_message, column_message, plane, shape(5 * SLOT, COLS)),
        in_specs=[SMEM] * 3 + [HBM] * 4 + [VMEM] * 3,
        out_specs=(VMEM,) * 4,
        scratch_shapes=level_scratch() + [flat] * 3 + [tile] * 2 + [transfers],
        compiler_params=PARAMS, cost_estimate=cost(30 * cells, 12 * cells), name="forcing",
    )(side_mix, vert_mix, thickness, tracer_one, tracer_two, east_flow, north_flow, depth_levels, corner_depth, diagonal)
    first_in, second_in = swap_both(first, second, "bx", n_bx, True)
    row_first, row_second, forcing, depth, diag, flux_left, flux_right = pl.pallas_call(
        columns_kernel,
        out_shape=(row_message, row_message, wide, wide, wide, shape(ROWS, 128), shape(ROWS, 128)),
        in_specs=[SMEM] * 2 + [VMEM] * 9,
        out_specs=(VMEM,) * 7,
        compiler_params=PARAMS, cost_estimate=cost(10**6, 10**6), name="columns",
    )(side_mix, thickness, first, second, first_in, second_in, forcing, depth_levels, corner_depth, diagonal, edge_rows)
    row_first_in, row_second_in = swap_both(row_first, row_second, "by", n_by, False)
    zero, one, two, sums, flux_rows = pl.pallas_call(
        solver_kernel,
        out_shape=(plane, plane, plane, shape(128, 128), shape(4 * SLOT, COLS)),
        in_specs=[SMEM] * 2 + [VMEM] * 7,
        out_specs=(VMEM,) * 5,
        compiler_params=PARAMS, cost_estimate=cost(4 * 10**6, 10**6), name="solver",
    )(side_mix, thickness, row_first, row_second, row_first_in, row_second_in, forcing, depth, diag)
    new_one, new_two = pl.pallas_call(
        tracers_kernel,
        out_shape=(shape(LEV, ROWS, COLS),) * 2,
        in_specs=[SMEM] * 2 + [HBM] * 4 + [VMEM] * 4,
        out_specs=(HBM,) * 2,
        scratch_shapes=level_scratch() + [pltpu.VMEM((LEV, ROWS, COLS), F32)] * 2
        + [transfers, pltpu.SemaphoreType.DMA((2, LEV // GROUP))],
        compiler_params=PARAMS, cost_estimate=cost(60 * cells, 20 * cells), name="tracers",
    )(side_mix, vert_mix, tracer_one, tracer_two, east_flow, north_flow, depth_levels, flux_left, flux_right, flux_rows)
    sums = lax.all_to_all(sums[:n_by * n_bx], ("by", "bx"), 0, 0, tiled=True)
    surface = pl.pallas_call(
        surface_kernel, out_shape=plane, in_specs=[VMEM] * 4, out_specs=VMEM,
        compiler_params=PARAMS, cost_estimate=cost(10**5, 10**5), name="surface",
    )(sums, zero, one, two)
    return new_one, new_two, surface


def solution(mesh):
    block, field = P(None, "by", "bx"), P("by", "bx")
    return jax.shard_map(
        on_device, mesh=mesh,
        in_specs=(block, block, block, block, field, P(), P(), P(), field, field),
        out_specs=(block, block, field), check_vma=False,
    )
```

```python
import jax
import jax.numpy as jnp
from jax import lax
from jax.experimental import pallas as pl
from jax.experimental.pallas import tpu as pltpu
from jax.sharding import PartitionSpec as P

LEV = 18
CHUNK = 16
SLOT = 24
ROWS, COLS = 64, 256
WIDE = COLS + 128
TALL = ROWS + 16
F32 = jnp.float32
VMEM = pl.BlockSpec(memory_space=pltpu.VMEM)
SMEM = pl.BlockSpec(memory_space=pltpu.SMEM)
HBM = pl.BlockSpec(memory_space=pl.ANY)
PARAMS = pltpu.CompilerParams(vmem_limit_bytes=16 * 1024 * 1024)


def iota(shape, axis):
    return lax.broadcasted_iota(jnp.int32, shape, axis)


def shape(*dims):
    return jax.ShapeDtypeStruct(dims, F32)


def pairs(size, odd, wrap):
    swaps = []
    for low in range(1 if odd else 0, size, 2):
        high = low + 1
        if high == size and not wrap:
            continue
        swaps += [(low, high % size), (high % size, low)]
    return swaps


def swap_both(first, second, axis, size, wrap):
    return (
        lax.ppermute(first, axis, pairs(size, False, wrap)),
        lax.ppermute(second, axis, pairs(size, True, wrap)),
    )


def by_side(axis, first, second):
    even = lax.axis_index(axis) % 2 == 0
    return jnp.where(even, first, second), jnp.where(even, second, first)


def load_chunks(sources, targets, sems):
    def copy(array, chunk):
        part = pl.ds(pl.multiple_of(chunk * CHUNK, CHUNK), CHUNK)
        return pltpu.make_async_copy(sources[array].at[:, part], targets[array].at[:, part], sems.at[array, chunk])

    return copy


def start_all(copies):
    for copy in copies:
        copy.start()


def wait_all(copies):
    for copy in copies:
        copy.wait()


def forcing_kernel(side_hbm, vert_hbm, thick_hbm, one_hbm, two_hbm, east_hbm, north_hbm, levels_hbm, corner_hbm, diag_hbm,
                   first_out, second_out, forcing_out, deep_out, depth_out, diag_out, edge_rows, weights,
                   side, vert, thick, one, two, east, north,
                   levels, corner, diag, east_deep, north_deep, east_sum, north_sum, column, right, left, sems, small):
    copy = load_chunks((one_hbm, two_hbm, east_hbm, north_hbm), (one, two, east, north), sems)
    chunks = ROWS // CHUNK
    pairs_of = ((levels_hbm, levels), (side_hbm, side), (vert_hbm, vert), (thick_hbm, thick), (corner_hbm, corner), (diag_hbm, diag))
    singles = [pltpu.make_async_copy(a, b, small.at[i]) for i, (a, b) in enumerate(pairs_of)]
    start_all(singles[:4])
    for chunk in range(chunks):
        start_all(copy(array, chunk) for array in range(4))
    start_all(singles[4:])
    wait_all(singles[:4])
    deep = levels[...]
    at_row, at_col = iota((ROWS, COLS), 0), iota((ROWS, COLS), 1)
    east_deep[...] = jnp.where(at_col < COLS - 1, jnp.minimum(deep, pltpu.roll(deep, COLS - 1, 1)), 0)
    north_deep[...] = jnp.where(at_row < ROWS - 1, jnp.minimum(deep, pltpu.roll(deep, ROWS - 1, 0)), 0)
    edge_rows[...] = jnp.zeros(edge_rows.shape, F32)
    row, lane = iota((CHUNK, COLS), 0), iota((CHUNK, 128), 1)
    wait_all(copy(array, 0) for array in range(4))

    @pl.loop(0, chunks)
    def _(chunk):
        @pl.when(chunk + 1 < chunks)
        def _():
            wait_all(copy(array, chunk + 1) for array in range(4))

        start = pl.multiple_of(chunk * CHUNK, CHUNK)
        part = pl.ds(start, CHUNK)
        here, to_east, to_north = levels[part], east_deep[part], north_deep[part]

        def level(k, carry):
            e_sum, n_sum, total, to_right, to_left = carry
            c_one, c_two = one[k, part], two[k, part]
            flow_e, flow_n = east[k, part].astype(F32), north[k, part].astype(F32)
            both = c_one - 0.5 * c_two
            beyond = one[k, pl.ds(start + CHUNK, 1)] - 0.5 * two[k, pl.ds(start + CHUNK, 1)]
            weight, mix = thick[k], side[k]
            below, above = jnp.minimum(k + 1, LEV - 1), jnp.maximum(k - 1, 0)
            fall = (weight - thick[below]) * vert[k]
            fall_above = (thick[above] - weight) * vert[above]
            total = total + both * jnp.where(
                here > k + 1, weight + fall_above - fall, jnp.where(here > k, weight + fall_above, 0.0))
            nxt = pltpu.roll(both, COLS - 1, 1)
            e_sum = e_sum + jnp.where(
                to_east > k, (0.5 * weight) * (flow_e * (both + nxt)) - (weight * mix) * (nxt - both), 0.0)
            nxt = jnp.where(row == CHUNK - 1, beyond, pltpu.roll(both, CHUNK - 1, 0))
            n_sum = n_sum + jnp.where(
                to_north > k, (0.5 * weight) * (flow_n * (both + nxt)) - (weight * mix) * (nxt - both), 0.0)
            to_right = jnp.where(lane == k, c_one[:, COLS - 1:], to_right)
            to_right = jnp.where(lane == k + LEV, c_two[:, COLS - 1:], to_right)
            to_right = jnp.where((lane == k + 2 * LEV) | (lane == k + 3 * LEV), flow_e[:, COLS - 1:], to_right)
            to_left = jnp.where(lane == k + 64, c_one[:, :1], to_left)
            to_left = jnp.where(lane == k + 64 + LEV, c_two[:, :1], to_left)
            return e_sum, n_sum, total, to_right, to_left

        flat, tile = jnp.zeros((CHUNK, COLS), F32), jnp.zeros((CHUNK, 128), F32)
        result = lax.fori_loop(0, LEV, level, (flat, flat, flat, tile, tile), unroll=3)
        for target, value in zip((east_sum, north_sum, column, right, left), result):
            target[part] = value

    @pl.loop(0, LEV)
    def _(k):
        edge_rows[pl.ds(k, 1)] = one[k, 0:1]
        edge_rows[pl.ds(SLOT + k, 1)] = two[k, 0:1]
        edge_rows[pl.ds(2 * SLOT + k, 1)] = one[k, ROWS - 1:ROWS]
        edge_rows[pl.ds(3 * SLOT + k, 1)] = two[k, ROWS - 1:ROWS]
        edge_rows[pl.ds(4 * SLOT + k, 1)] = north[k, ROWS - CHUNK:ROWS].astype(F32)[CHUNK - 1:]

    at, level = iota((8, 128), 1), iota((SLOT, 128), 0)
    lane_mix = lane_weight = jnp.zeros((8, 128), F32)
    row_mix = row_weight = jnp.zeros((SLOT, 128), F32)
    for k in range(LEV):
        lane_mix = jnp.where((at == k) | (at == k + LEV), side[k], lane_mix)
        lane_weight = jnp.where(at == k, thick[k], jnp.where(at == k + LEV, -0.5 * thick[k], lane_weight))
        row_mix = jnp.where(level == k, side[k], row_mix)
        row_weight = jnp.where(level == k, thick[k], row_weight)
    weights[...] = jnp.concatenate([lane_mix, lane_weight, row_mix, row_weight], axis=0)
    e_sum, n_sum = east_sum[...], north_sum[...]
    forcing = column[...] - (e_sum - pltpu.roll(e_sum, 1, 1)) - (n_sum - pltpu.roll(n_sum, 1, 0))
    forcing_out[...] = forcing
    wait_all(singles[4:])
    depth = jnp.where(deep > 0, corner[...], 0.0)
    fields = (forcing, depth, diag[...], deep.astype(F32))
    deep_out[...], depth_out[...], diag_out[...] = fields[3], fields[1], fields[2]
    to_right, to_left = right[...], left[...]
    lane = iota((ROWS, 128), 1)
    for i, field in enumerate(fields):
        tile = field[:, COLS - 128:]
        tile = pltpu.roll(tile, 128 - 2 * i, 1) if i else tile
        to_right = jnp.where((lane >= 126 - 2 * i) & (lane < 128 - 2 * i), tile, to_right)
        tile = field[:, :128]
        tile = pltpu.roll(tile, 3 * i, 1) if i else tile
        to_left = jnp.where((lane >= 3 * i) & (lane < 3 * i + 3), tile, to_left)
    rows_0 = edge_rows[0:SLOT] - 0.5 * edge_rows[SLOT:2 * SLOT]
    rows_1 = edge_rows[2 * SLOT:3 * SLOT] - 0.5 * edge_rows[3 * SLOT:4 * SLOT]
    rows_2 = edge_rows[4 * SLOT:5 * SLOT]
    lane = iota((SLOT, 128), 1)
    corner_right = corner_left = jnp.zeros((SLOT, 128), F32)
    for i, rows in enumerate((rows_0, rows_1, rows_2)):
        tile = rows[:, COLS - 128:]
        tile = pltpu.roll(tile, 128 - 2 * i, 1) if i else tile
        corner_right = jnp.where((lane >= 126 - 2 * i) & (lane < 128 - 2 * i), tile, corner_right)
        tile = rows[:, :128]
        tile = pltpu.roll(tile, 3 * i, 1) if i else tile
        corner_left = jnp.where((lane >= 3 * i) & (lane < 3 * i + 3), tile, corner_left)
    even = lax.axis_index("bx") % 2 == 0
    first_out[:ROWS] = jnp.where(even, to_right, to_left)
    second_out[:ROWS] = jnp.where(even, to_left, to_right)
    first_out[ROWS:] = jnp.where(even, corner_right, corner_left)
    second_out[ROWS:] = jnp.where(even, corner_left, corner_right)


def lane_tile(from_right, from_left, i):
    lane = iota(from_right.shape, 1)
    if i:
        from_right, from_left = pltpu.roll(from_right, 128 - 3 * i, 1), pltpu.roll(from_left, 2 * i, 1)
    return jnp.where(lane < 3, from_right, jnp.where(lane >= 126, from_left, 0.0))


def columns_kernel(weights, first, second, first_in, second_in, forcing, deep_in, depth_in, diag, edge_rows,
                   first_out, second_out, forcing_wide, depth_wide, diag_wide, flux_left, flux_right):
    own_right, own_left = by_side("bx", first[...], second[...])
    from_right, from_left = by_side("bx", first_in[...], second_in[...])
    deep_f, depth = deep_in[...], depth_in[...]
    lane = iota((ROWS, 128), 1)
    at = iota((8, 128), 1)
    mix, weight = weights[0:1], weights[8:9]
    of_lane = jnp.where(at < LEV, at, jnp.where(at < 2 * LEV, at - LEV, 100))[:1].astype(F32)

    def face(west, east, flow, west_deep, east_deep):
        flux = 0.5 * flow * (west + east) - mix * (east - west)
        flux = jnp.where(of_lane < jnp.minimum(west_deep, east_deep), flux, 0.0)
        return flux, jnp.sum(flux * weight, axis=1, keepdims=True)

    own, seen = own_left[:ROWS], from_left[:ROWS]
    flux, west_sum = face(seen, pltpu.roll(own, 64, 1), pltpu.roll(seen, 128 - 2 * LEV, 1), seen[:, 121:122], deep_f[:, :1])
    flux_left[...] = flux
    own, seen = own_right[:ROWS], from_right[:ROWS]
    flux, east_sum = face(own, pltpu.roll(seen, 64, 1), pltpu.roll(own, 128 - 2 * LEV, 1), deep_f[:, COLS - 1:], seen[:, 9:10])
    flux_right[...] = flux

    mine = forcing[...]
    tiles = (
        mine[:, :128] + jnp.where(lane == 0, west_sum, 0.0),
        mine[:, 128:] - jnp.where(lane == 127, east_sum, 0.0),
        lane_tile(from_right[:ROWS], from_left[:ROWS], 0)
        + jnp.where(lane == 0, east_sum, jnp.where(lane == 127, -west_sum, 0.0)),
    )
    wide = jnp.concatenate(tiles, axis=1)
    forcing_wide[...] = wide
    depth_w = jnp.concatenate([depth, lane_tile(from_right[:ROWS], from_left[:ROWS], 1)], axis=1)
    diag_w = jnp.concatenate([diag[...], lane_tile(from_right[:ROWS], from_left[:ROWS], 2)], axis=1)
    deep_w = jnp.concatenate([deep_f, lane_tile(from_right[:ROWS], from_left[:ROWS], 3)], axis=1)
    depth_wide[...] = depth_w
    diag_wide[...] = diag_w

    def rows(value, i):
        return jnp.concatenate([value, lane_tile(from_right[ROWS:], from_left[ROWS:], i)], axis=1)

    nothing = jnp.zeros((SLOT, 128), F32)
    two_0, two_1 = edge_rows[SLOT:2 * SLOT], edge_rows[3 * SLOT:4 * SLOT]
    both_0 = rows(edge_rows[0:SLOT] - 0.5 * two_0, 0)
    both_1 = rows(edge_rows[2 * SLOT:3 * SLOT] - 0.5 * two_1, 1)
    north_1 = rows(edge_rows[4 * SLOT:5 * SLOT], 2)
    even = lax.axis_index("by") % 2 == 0
    up = (both_1, jnp.concatenate([two_1, nothing], axis=1), north_1, jnp.concatenate(
        [wide[62:64], deep_w[63:64], depth_w[62:64], diag_w[63:64], jnp.zeros((2, WIDE), F32)], axis=0))
    down = (both_0, jnp.concatenate([two_0, nothing], axis=1), jnp.zeros((SLOT, WIDE), F32), jnp.concatenate(
        [wide[0:3], deep_w[0:1], depth_w[0:2], diag_w[0:2]], axis=0))
    for i in range(4):
        place = slice(i * SLOT, i * SLOT + (SLOT if i < 3 else 8))
        first_out[place] = jnp.where(even, up[i], down[i])
        second_out[place] = jnp.where(even, down[i], up[i])


def operate(field, half_depth, diag):
    east = pltpu.roll(field, WIDE - 1, 1)
    north = pltpu.roll(field, TALL - 1, 0)
    corner = pltpu.roll(north, WIDE - 1, 1)
    plus = half_depth * (corner - field)
    minus = half_depth * (east - north)
    return (diag * field - plus + pltpu.roll(minus, 1, 1)
            + pltpu.roll(pltpu.roll(plus, 1, 1) - minus, 1, 0)), plus, minus


def solver_kernel(weights, first, second, first_in, second_in, forcing, depth, diag,
                  low_one, low_two, high_one, high_two, tracer_one, tracer_two,
                  zero_out, one_out, two_out, sums_out, full_one, full_two, strips, sems):
    own_up, own_down = by_side("by", first[...], second[...])
    above, beneath = by_side("by", first_in[...], second_in[...])
    level = iota((SLOT, WIDE), 0)
    mix, weight = (jnp.concatenate([weights[i:i + SLOT]] * (WIDE // 128), axis=1) for i in (16, 16 + SLOT))
    level_f = level.astype(F32)

    def face(south, north, south_deep, north_deep):
        flow = south[2 * SLOT:3 * SLOT]
        wet = level_f < jnp.minimum(south_deep, north_deep)

        def flux(low, high):
            columns = low.shape[1]
            value = 0.5 * flow[:, :columns] * (low + high) - mix[:, :columns] * (high - low)
            return jnp.where(wet[:, :columns], value, 0.0)

        both = flux(south[:SLOT], north[:SLOT])
        two = flux(south[SLOT:2 * SLOT, :COLS], north[SLOT:2 * SLOT, :COLS])
        return jnp.sum(both * weight, axis=0, keepdims=True), both[:, :COLS] + 0.5 * two, two

    top, top_one, top_two = face(own_up, above, own_up[74:75], above[75:76])
    bottom, bottom_one, bottom_two = face(beneath, own_down, beneath[74:75], own_down[75:76])

    strip_row = iota((8, COLS), 0)
    stores = []
    for i, (strip, flux, at, target) in enumerate((
            (low_one, bottom_one, 0, full_one), (low_two, bottom_two, 0, full_two),
            (high_one, -top_one, 7, full_one), (high_two, -top_two, 7, full_two))):
        for k in range(LEV):
            strips[i, k] = strip[k] + jnp.where(strip_row == at, flux[k:k + 1], 0.0)
        place = pl.ds(0 if at == 0 else ROWS - 8, 8)
        stores.append(pltpu.make_async_copy(strips.at[i], target.at[:, place], sems.at[i]))
        stores[-1].start()

    def blank(count):
        return jnp.zeros((count, WIDE), F32)

    own_row = iota((ROWS, WIDE), 0)
    mine = forcing[...] + jnp.where(own_row == 0, bottom, jnp.where(own_row == ROWS - 1, -top, 0.0))
    field = jnp.concatenate([
        jnp.concatenate([blank(6), beneath[72:73], beneath[73:74] - bottom], axis=0), mine,
        jnp.concatenate([above[72:73] + top, above[73:75], blank(5)], axis=0)], axis=0)
    half_depth = 0.5 * jnp.concatenate([
        jnp.concatenate([blank(6), beneath[75:77]], axis=0), depth[...],
        jnp.concatenate([above[76:78], blank(6)], axis=0)], axis=0)
    diag_all = jnp.concatenate([
        jnp.concatenate([blank(7), beneath[77:78]], axis=0), diag[...],
        jnp.concatenate([above[78:80], blank(6)], axis=0)], axis=0)
    last = lax.axis_index("by") == lax.axis_size("by") - 1
    inside = iota((TALL, WIDE), 0) < jnp.where(last, ROWS + 8, TALL)

    image, _, _ = operate(field, half_depth, diag_all)
    image = jnp.where(inside, image, 0.0)
    twice, _, _ = operate(image, half_depth, diag_all)
    twice = jnp.where(inside, twice, 0.0)
    _, plus, minus = operate(twice, half_depth, diag_all)
    east = pltpu.roll(twice, WIDE - 1, 1)
    north = pltpu.roll(twice, TALL - 1, 0)
    corner = pltpu.roll(north, WIDE - 1, 1)
    energy = diag_all * twice * twice + plus * (corner - twice) + minus * (east - north)

    def own(value):
        return value[8:8 + ROWS, :COLS]

    v_0, v_1, v_2 = own(field), own(image), own(twice)
    zero_out[...], one_out[...], two_out[...] = v_0, v_1, v_2
    lane = iota((128, 128), 1)
    sums = jnp.zeros((128, 128), F32)
    for i, product in enumerate((v_0 * v_0, v_0 * v_1, v_1 * v_1, v_1 * v_2, v_2 * v_2, own(energy))):
        sums = jnp.where(lane == i, jnp.sum(product, keepdims=True), sums)
    sums_out[...] = sums
    wait_all(stores)


def surface_kernel(sums, zero, one, two, surface):
    total = jnp.sum(sums[...], axis=0, keepdims=True)
    m = [total[:, i:i + 1] for i in range(6)]
    a_0 = m[0] / m[1]
    rr_1 = m[0] - 2.0 * a_0 * m[1] + a_0 * a_0 * m[2]
    rar_1 = m[1] - 2.0 * a_0 * m[2] + a_0 * a_0 * m[3]
    b_1 = rr_1 / m[0]
    a_1 = rr_1 / (rar_1 - b_1 * rr_1 / a_0)
    grow = 1.0 + b_1
    p_1 = -(a_0 + a_1 * grow)
    p_2 = a_1 * a_0
    rr_2 = m[0] + p_1 * p_1 * m[2] + p_2 * p_2 * m[4] + 2.0 * (p_1 * m[1] + p_2 * m[2] + p_1 * p_2 * m[3])
    rar_2 = m[1] + p_1 * p_1 * m[3] + p_2 * p_2 * m[5] + 2.0 * (p_1 * m[2] + p_2 * m[3] + p_1 * p_2 * m[4])
    b_2 = rr_2 / rr_1
    a_2 = rr_2 / (rar_2 - b_2 * rr_2 / a_1)
    w_0 = a_0 + a_1 * grow + a_2 * (1.0 + b_2 * grow)
    w_1 = -a_1 * a_0 + a_2 * (p_1 - b_2 * a_0)
    w_2 = a_2 * p_2
    surface[...] = w_0 * zero[...] + w_1 * one[...] + w_2 * two[...]


def tracers_kernel(side_hbm, vert_hbm, one_hbm, two_hbm, east_hbm, north_hbm, deep_in, flux_left, flux_right,
                   one_out, two_out, low_one, low_two, high_one, high_two,
                   side, vert, one, two, east, north, east_deep, north_deep, new_one, new_two, edge, sems, small, out_sems):
    copy = load_chunks((one_hbm, two_hbm, east_hbm, north_hbm), (one, two, east, north), sems)
    chunks = ROWS // CHUNK
    singles = [pltpu.make_async_copy(a, b, small.at[i]) for i, (a, b) in enumerate(((side_hbm, side), (vert_hbm, vert)))]
    start_all(singles)
    for chunk in range(chunks):
        start_all(copy(array, chunk) for array in range(4))

    kept = ((0, 8, 8), (1, CHUNK, CHUNK), (2, 2 * CHUNK, CHUNK), (3, 3 * CHUNK, 8))

    def store(array, which):
        chunk, start, count = kept[which]
        source, target = ((new_one, one_out), (new_two, two_out))[array]
        return pltpu.make_async_copy(
            source.at[:, pl.ds(start, count)], target.at[:, pl.ds(start, count)], out_sems.at[array, which])

    deep = deep_in[...].astype(jnp.int32)
    at_row = iota((ROWS, COLS), 0)
    east_deep[...] = jnp.minimum(deep, pltpu.roll(deep, COLS - 1, 1))
    north_deep[...] = jnp.where(at_row < ROWS - 1, jnp.minimum(deep, pltpu.roll(deep, ROWS - 1, 0)), 0)
    edge[...] = jnp.zeros(edge.shape, F32)
    row, lane = iota((CHUNK, COLS), 0), iota((CHUNK, 128), 1)
    wait_all(singles)
    wait_all(copy(array, 0) for array in range(4))

    @pl.loop(0, chunks)
    def _(chunk):
        @pl.when(chunk + 1 < chunks)
        def _():
            wait_all(copy(array, chunk + 1) for array in range(4))

        start = pl.multiple_of(chunk * CHUNK, CHUNK)
        part = pl.ds(start, CHUNK)
        here = deep_in[part].astype(jnp.int32)
        to_east, to_north = east_deep[part], north_deep[part]
        west_flux, east_flux = flux_left[part], flux_right[part]

        def level(k, falls):
            flow_e, flow_n = 0.5 * east[k, part].astype(F32), 0.5 * north[k, part].astype(F32)
            mix, fall_w = side[k], vert[k]
            below = jnp.minimum(k + 1, LEV - 1)
            wet, wet_below = here > k, here > k + 1
            wet_east, wet_north = to_east > k, to_north > k
            kept_falls = []
            for i, (source, target) in enumerate(((one, new_one), (two, new_two))):
                c = source[k, part]
                nxt = pltpu.roll(c, COLS - 1, 1)
                e = jnp.where(wet_east, flow_e * (c + nxt) - mix * (nxt - c), 0.0)
                seam = pltpu.roll(east_flux, 127 - k - i * LEV, 1)
                e = jnp.concatenate([e[:, :128], jnp.where(lane == 127, seam, e[:, 128:])], axis=1)
                e_west = pltpu.roll(e, 1, 1)
                seam = pltpu.roll(west_flux, lax.rem(256 - k - i * LEV, 128), 1)
                e_west = jnp.concatenate([jnp.where(lane == 0, seam, e_west[:, :128]), e_west[:, 128:]], axis=1)
                nxt = jnp.where(row == CHUNK - 1, source[k, pl.ds(start + CHUNK, 1)], pltpu.roll(c, CHUNK - 1, 0))
                n = jnp.where(wet_north, flow_n * (c + nxt) - mix * (nxt - c), 0.0)
                place = pl.ds(i * SLOT + k, 1)
                n_south = jnp.where(row == 0, edge[place], pltpu.roll(n, 1, 0))
                edge[place] = n[CHUNK - 1:]
                fall = jnp.where(wet_below, fall_w * (source[below, part] - c), 0.0)
                target[k, part] = jnp.where(wet, c - (e - e_west) - (n - n_south) + (fall - falls[i]), 0.0)
                kept_falls.append(fall)
            return tuple(kept_falls)

        nothing = jnp.zeros((CHUNK, COLS), F32)
        lax.fori_loop(0, LEV, level, (nothing, nothing), unroll=2)
        for which in range(chunks):
            @pl.when(chunk == which)
            def _():
                store(0, which).start()
                store(1, which).start()

    low_one[...], low_two[...] = new_one[:, :8], new_two[:, :8]
    high_one[...], high_two[...] = new_one[:, ROWS - 8:], new_two[:, ROWS - 8:]
    wait_all(store(array, which) for array in range(2) for which in range(chunks))


def level_scratch():
    block, taller = (LEV, ROWS, COLS), (LEV, ROWS + 8, COLS)
    return [pltpu.VMEM(taller, F32), pltpu.VMEM(taller, F32), pltpu.VMEM(block, jnp.bfloat16), pltpu.VMEM(block, jnp.bfloat16)]


def cost(flops, moved):
    return pl.CostEstimate(flops=flops, bytes_accessed=moved, transcendentals=0)


def on_device(*arrays):
    (tracer_one, tracer_two, east_flow, north_flow, depth_levels, side_mix, vert_mix, thickness,
     corner_depth, diagonal) = (pltpu.with_memory_space_constraint(array, pltpu.HBM) for array in arrays)
    n_by, n_bx = lax.axis_size("by"), lax.axis_size("bx")
    cells = LEV * ROWS * COLS
    plane, wide, tile = shape(ROWS, COLS), shape(ROWS, WIDE), shape(ROWS, 128)
    block, strip = shape(LEV, ROWS, COLS), shape(LEV, 8, COLS)
    column_message, row_message = shape(ROWS + SLOT, 128), shape(3 * SLOT + 8, WIDE)
    flat, flat_int = pltpu.VMEM((ROWS, COLS), F32), pltpu.VMEM((ROWS, COLS), jnp.int32)
    level_list = pltpu.SMEM((LEV,), F32)
    transfers = pltpu.SemaphoreType.DMA((4, ROWS // CHUNK))
    first, second, forcing, deep, depth, diag, edge_rows, weights = pl.pallas_call(
        forcing_kernel,
        out_shape=(column_message, column_message, plane, plane, plane, plane, shape(5 * SLOT, COLS), tile),
        in_specs=[HBM] * 10,
        out_specs=(VMEM,) * 8,
        scratch_shapes=[level_list] * 3 + level_scratch() + [flat_int, flat, flat] + [flat_int] * 2 + [flat] * 3
        + [pltpu.VMEM((ROWS, 128), F32)] * 2 + [transfers, pltpu.SemaphoreType.DMA((6,))],
        compiler_params=PARAMS, cost_estimate=cost(30 * cells, 12 * cells), name="forcing",
    )(side_mix, vert_mix, thickness, tracer_one, tracer_two, east_flow, north_flow, depth_levels, corner_depth, diagonal)
    first_in, second_in = swap_both(first, second, "bx", n_bx, True)
    row_first, row_second, forcing, depth, diag, flux_left, flux_right = pl.pallas_call(
        columns_kernel,
        out_shape=(row_message, row_message, wide, wide, wide, tile, tile),
        in_specs=[VMEM] * 10,
        out_specs=(VMEM,) * 7,
        compiler_params=PARAMS, cost_estimate=cost(10**6, 10**6), name="columns",
    )(weights, first, second, first_in, second_in, forcing, deep, depth, diag, edge_rows)
    row_first_in, row_second_in = swap_both(row_first, row_second, "by", n_by, False)
    part_one, part_two, low_one, low_two, high_one, high_two = pl.pallas_call(
        tracers_kernel,
        out_shape=(block, block, strip, strip, strip, strip),
        in_specs=[HBM] * 6 + [VMEM] * 3,
        out_specs=(HBM,) * 2 + (VMEM,) * 4,
        scratch_shapes=[level_list] * 2 + level_scratch() + [flat_int] * 2 + [pltpu.VMEM((LEV, ROWS, COLS), F32)] * 2
        + [pltpu.VMEM((2 * SLOT, COLS), F32), transfers, pltpu.SemaphoreType.DMA((2,)),
           pltpu.SemaphoreType.DMA((2, ROWS // CHUNK))],
        compiler_params=PARAMS, cost_estimate=cost(60 * cells, 20 * cells), name="tracers",
    )(side_mix, vert_mix, tracer_one, tracer_two, east_flow, north_flow, deep, flux_left, flux_right)
    zero, one, two, sums, new_one, new_two = pl.pallas_call(
        solver_kernel,
        out_shape=(plane, plane, plane, shape(128, 128), block, block),
        in_specs=[VMEM] * 12 + [HBM] * 2,
        out_specs=(VMEM,) * 4 + (HBM,) * 2,
        input_output_aliases={12: 4, 13: 5},
        scratch_shapes=[pltpu.VMEM((4, LEV, 8, COLS), F32), pltpu.SemaphoreType.DMA((4,))],
        compiler_params=PARAMS, cost_estimate=cost(4 * 10**6, 10**6), name="solver",
    )(weights, row_first, row_second, row_first_in, row_second_in, forcing, depth, diag,
      low_one, low_two, high_one, high_two, part_one, part_two)
    sums = lax.all_to_all(sums[:n_by * n_bx], ("by", "bx"), 0, 0, tiled=True)
    surface = pl.pallas_call(
        surface_kernel, out_shape=plane, in_specs=[VMEM] * 4, out_specs=VMEM,
        compiler_params=PARAMS, cost_estimate=cost(10**5, 10**5), name="surface",
    )(sums, zero, one, two)
    return new_one, new_two, surface


def solution(mesh):
    block, field = P(None, "by", "bx"), P("by", "bx")
    return jax.shard_map(
        on_device, mesh=mesh,
        in_specs=(block, block, block, block, field, P(), P(), P(), field, field),
        out_specs=(block, block, field), check_vma=False,
    )
```

```python
import jax
import jax.numpy as jnp
from jax import lax
from jax.experimental import pallas as pl
from jax.experimental.pallas import tpu as pltpu
from jax.sharding import PartitionSpec as P

LEV = 18
AHEAD = 4
CHUNK = 16
SLOT = 24
ROWS, COLS = 64, 256
WIDE = COLS + 128
TALL = ROWS + 16
FORCING_UNROLL = 18
TRACERS_UNROLL = 6
F32 = jnp.float32
VMEM = pl.BlockSpec(memory_space=pltpu.VMEM)
SMEM = pl.BlockSpec(memory_space=pltpu.SMEM)
HBM = pl.BlockSpec(memory_space=pl.ANY)
PARAMS = pltpu.CompilerParams(vmem_limit_bytes=16 * 1024 * 1024)


def iota(shape, axis):
    return lax.broadcasted_iota(jnp.int32, shape, axis)


def shape(*dims):
    return jax.ShapeDtypeStruct(dims, F32)


def pairs(size, odd, wrap):
    swaps = []
    for low in range(1 if odd else 0, size, 2):
        high = low + 1
        if high == size and not wrap:
            continue
        swaps += [(low, high % size), (high % size, low)]
    return swaps


def swap_both(first, second, axis, size, wrap):
    return (
        lax.ppermute(first, axis, pairs(size, False, wrap)),
        lax.ppermute(second, axis, pairs(size, True, wrap)),
    )


def by_side(axis, first, second):
    even = lax.axis_index(axis) % 2 == 0
    return jnp.where(even, first, second), jnp.where(even, second, first)


def load_chunks(sources, targets, sems):
    def copy(array, chunk):
        part = pl.ds(pl.multiple_of(chunk * CHUNK, CHUNK), CHUNK)
        return pltpu.make_async_copy(sources[array].at[:, part], targets[array].at[:, part], sems.at[array, chunk])

    return copy


def start_all(copies):
    for copy in copies:
        copy.start()


def wait_all(copies):
    for copy in copies:
        copy.wait()


def forcing_kernel(side_hbm, vert_hbm, thick_hbm, one_hbm, two_hbm, east_hbm, north_hbm, levels_hbm, corner_hbm, diag_hbm,
                   first_out, second_out, forcing_out, deep_out, depth_out, diag_out, edge_rows, weights,
                   one, two, east, north, side, vert, thick, levels, corner, diag, east_deep, north_deep, east_sum, north_sum, column, right, left, sems, small):
    copy = load_chunks((one_hbm, two_hbm, east_hbm, north_hbm), (one, two, east, north), sems)
    chunks = ROWS // CHUNK
    pairs_of = ((levels_hbm, levels), (side_hbm, side), (vert_hbm, vert), (thick_hbm, thick), (corner_hbm, corner), (diag_hbm, diag))
    singles = [pltpu.make_async_copy(a, b, small.at[i]) for i, (a, b) in enumerate(pairs_of)]
    start_all(singles[:4])
    for chunk in range(AHEAD):
        start_all(copy(array, chunk) for array in range(4))
    start_all(singles[4:])
    for array in (one, two):
        array[:, ROWS:] = jnp.zeros((LEV, 8, COLS), F32)
    wait_all(singles[:4])
    deep = levels[...]
    at_row, at_col = iota((ROWS, COLS), 0), iota((ROWS, COLS), 1)
    east_deep[...] = jnp.where(at_col < COLS - 1, jnp.minimum(deep, pltpu.roll(deep, COLS - 1, 1)), 0)
    north_deep[...] = jnp.where(at_row < ROWS - 1, jnp.minimum(deep, pltpu.roll(deep, ROWS - 1, 0)), 0)
    edge_rows[...] = jnp.zeros(edge_rows.shape, F32)
    row, lane = iota((CHUNK, COLS), 0), iota((CHUNK, 128), 1)
    wait_all(copy(array, 0) for array in range(4))

    @pl.loop(0, chunks)
    def _(chunk):
        @pl.when(chunk + 1 < chunks)
        def _():
            wait_all(copy(array, chunk + 1) for array in range(4))

        @pl.when(chunk + AHEAD < chunks)
        def _():
            start_all(copy(array, chunk + AHEAD) for array in range(4))

        start = pl.multiple_of(chunk * CHUNK, CHUNK)
        part = pl.ds(start, CHUNK)
        here, to_east, to_north = levels[part], east_deep[part], north_deep[part]

        def level(k, carry):
            e_sum, n_sum, total, to_right, to_left = carry
            c_one, c_two = one[k, part], two[k, part]
            flow_e, flow_n = east[k, part].astype(F32), north[k, part].astype(F32)
            both = c_one - 0.5 * c_two
            beyond = one[k, pl.ds(start + CHUNK, 1)] - 0.5 * two[k, pl.ds(start + CHUNK, 1)]
            weight, mix = thick[k], 2.0 * side[k]
            below, above = jnp.minimum(k + 1, LEV - 1), jnp.maximum(k - 1, 0)
            fall = (weight - thick[below]) * vert[k]
            fall_above = (thick[above] - weight) * vert[above]
            total = total + both * jnp.where(
                here > k + 1, weight + fall_above - fall, jnp.where(here > k, weight + fall_above, 0.0))
            both, beyond = (0.5 * weight) * both, (0.5 * weight) * beyond
            nxt = pltpu.roll(both, COLS - 1, 1)
            e_sum = e_sum + jnp.where(to_east > k, flow_e * (both + nxt) - mix * (nxt - both), 0.0)
            nxt = jnp.where(row == CHUNK - 1, beyond, pltpu.roll(both, CHUNK - 1, 0))
            n_sum = n_sum + jnp.where(to_north > k, flow_n * (both + nxt) - mix * (nxt - both), 0.0)
            to_right = jnp.where(lane == k, c_one[:, COLS - 1:], to_right)
            to_right = jnp.where(lane == k + LEV, c_two[:, COLS - 1:], to_right)
            to_right = jnp.where((lane == k + 2 * LEV) | (lane == k + 3 * LEV), flow_e[:, COLS - 1:], to_right)
            to_left = jnp.where(lane == k + 64, c_one[:, :1], to_left)
            to_left = jnp.where(lane == k + 64 + LEV, c_two[:, :1], to_left)
            return e_sum, n_sum, total, to_right, to_left

        flat, tile = jnp.zeros((CHUNK, COLS), F32), jnp.zeros((CHUNK, 128), F32)
        result = lax.fori_loop(0, LEV, level, (flat, flat, flat, tile, tile), unroll=FORCING_UNROLL)
        for target, value in zip((east_sum, north_sum, column, right, left), result):
            target[part] = value

    for k in range(LEV):
        rows = (one[k, 0:1], two[k, 0:1], one[k, ROWS - 1:ROWS], two[k, ROWS - 1:ROWS],
                north[k, ROWS - 16:ROWS].astype(F32)[15:])
        for i, value in enumerate(rows):
            edge_rows[i * SLOT + k:i * SLOT + k + 1] = value

    at, level = iota((8, COLS), 1), iota((SLOT, COLS), 0)
    lane_mix = lane_weight = jnp.zeros((8, COLS), F32)
    row_mix = row_weight = row_vert = jnp.zeros((SLOT, COLS), F32)
    for k in range(LEV):
        lane_mix = jnp.where((at == k) | (at == k + LEV), side[k], lane_mix)
        lane_weight = jnp.where(at == k, thick[k], jnp.where(at == k + LEV, -0.5 * thick[k], lane_weight))
        row_mix = jnp.where(level == k, side[k], row_mix)
        row_weight = jnp.where(level == k, thick[k], row_weight)
        row_vert = jnp.where(level == k, vert[k], row_vert)
    weights[...] = jnp.concatenate([lane_mix, lane_weight, row_mix, row_weight, row_vert], axis=0)
    e_sum, n_sum = east_sum[...], north_sum[...]
    forcing = column[...] - (e_sum - pltpu.roll(e_sum, 1, 1)) - (n_sum - pltpu.roll(n_sum, 1, 0))
    forcing_out[...] = forcing
    wait_all(singles[4:])
    depth = jnp.where(deep > 0, corner[...], 0.0)
    fields = (forcing, depth, diag[...], deep.astype(F32))
    deep_out[...], depth_out[...], diag_out[...] = fields[3], fields[1], fields[2]
    to_right, to_left = right[...], left[...]
    lane = iota((ROWS, 128), 1)
    for i, field in enumerate(fields):
        tile = field[:, COLS - 128:]
        tile = pltpu.roll(tile, 128 - 2 * i, 1) if i else tile
        to_right = jnp.where((lane >= 126 - 2 * i) & (lane < 128 - 2 * i), tile, to_right)
        tile = field[:, :128]
        tile = pltpu.roll(tile, 3 * i, 1) if i else tile
        to_left = jnp.where((lane >= 3 * i) & (lane < 3 * i + 3), tile, to_left)
    rows_0 = edge_rows[0:SLOT] - 0.5 * edge_rows[SLOT:2 * SLOT]
    rows_1 = edge_rows[2 * SLOT:3 * SLOT] - 0.5 * edge_rows[3 * SLOT:4 * SLOT]
    rows_2 = edge_rows[4 * SLOT:5 * SLOT]
    lane = iota((SLOT, 128), 1)
    corner_right = corner_left = jnp.zeros((SLOT, 128), F32)
    for i, rows in enumerate((rows_0, rows_1, rows_2)):
        tile = rows[:, COLS - 128:]
        tile = pltpu.roll(tile, 128 - 2 * i, 1) if i else tile
        corner_right = jnp.where((lane >= 126 - 2 * i) & (lane < 128 - 2 * i), tile, corner_right)
        tile = rows[:, :128]
        tile = pltpu.roll(tile, 3 * i, 1) if i else tile
        corner_left = jnp.where((lane >= 3 * i) & (lane < 3 * i + 3), tile, corner_left)
    even = lax.axis_index("bx") % 2 == 0
    first_out[:ROWS] = jnp.where(even, to_right, to_left)
    second_out[:ROWS] = jnp.where(even, to_left, to_right)
    first_out[ROWS:] = jnp.where(even, corner_right, corner_left)
    second_out[ROWS:] = jnp.where(even, corner_left, corner_right)


def lane_tile(from_right, from_left, i):
    lane = iota(from_right.shape, 1)
    if i:
        from_right, from_left = pltpu.roll(from_right, 128 - 3 * i, 1), pltpu.roll(from_left, 2 * i, 1)
    return jnp.where(lane < 3, from_right, jnp.where(lane >= 126, from_left, 0.0))


def columns_kernel(weights, first, second, first_in, second_in, forcing, deep_in, depth_in, diag, edge_rows,
                   first_out, second_out, forcing_wide, depth_wide, diag_wide, flux_left, flux_right):
    own_right, own_left = by_side("bx", first[...], second[...])
    from_right, from_left = by_side("bx", first_in[...], second_in[...])
    deep_f, depth = deep_in[...], depth_in[...]
    lane = iota((ROWS, 128), 1)
    at = iota((8, 128), 1)
    mix, weight = weights[0:1, :128], weights[8:9, :128]
    of_lane = jnp.where(at < LEV, at, jnp.where(at < 2 * LEV, at - LEV, 100))[:1].astype(F32)

    def face(west, east, flow, west_deep, east_deep):
        flux = 0.5 * flow * (west + east) - mix * (east - west)
        flux = jnp.where(of_lane < jnp.minimum(west_deep, east_deep), flux, 0.0)
        return flux, jnp.sum(flux * weight, axis=1, keepdims=True)

    own, seen = own_left[:ROWS], from_left[:ROWS]
    flux, west_sum = face(seen, pltpu.roll(own, 64, 1), pltpu.roll(seen, 128 - 2 * LEV, 1), seen[:, 121:122], deep_f[:, :1])
    flux_left[...] = 2.0 * flux
    own, seen = own_right[:ROWS], from_right[:ROWS]
    flux, east_sum = face(own, pltpu.roll(seen, 64, 1), pltpu.roll(own, 128 - 2 * LEV, 1), deep_f[:, COLS - 1:], seen[:, 9:10])
    flux_right[...] = 2.0 * flux

    mine = forcing[...]
    tiles = (
        mine[:, :128] + jnp.where(lane == 0, west_sum, 0.0),
        mine[:, 128:] - jnp.where(lane == 127, east_sum, 0.0),
        lane_tile(from_right[:ROWS], from_left[:ROWS], 0)
        + jnp.where(lane == 0, east_sum, jnp.where(lane == 127, -west_sum, 0.0)),
    )
    wide = jnp.concatenate(tiles, axis=1)
    forcing_wide[...] = wide
    depth_w = jnp.concatenate([depth, lane_tile(from_right[:ROWS], from_left[:ROWS], 1)], axis=1)
    diag_w = jnp.concatenate([diag[...], lane_tile(from_right[:ROWS], from_left[:ROWS], 2)], axis=1)
    deep_w = jnp.concatenate([deep_f, lane_tile(from_right[:ROWS], from_left[:ROWS], 3)], axis=1)
    depth_wide[...] = depth_w
    diag_wide[...] = diag_w

    def rows(value, i):
        return jnp.concatenate([value, lane_tile(from_right[ROWS:], from_left[ROWS:], i)], axis=1)

    nothing = jnp.zeros((SLOT, 128), F32)
    two_0, two_1 = edge_rows[SLOT:2 * SLOT], edge_rows[3 * SLOT:4 * SLOT]
    both_0 = rows(edge_rows[0:SLOT] - 0.5 * two_0, 0)
    both_1 = rows(edge_rows[2 * SLOT:3 * SLOT] - 0.5 * two_1, 1)
    north_1 = rows(edge_rows[4 * SLOT:5 * SLOT], 2)
    even = lax.axis_index("by") % 2 == 0
    up = (both_1, jnp.concatenate([two_1, nothing], axis=1), north_1, jnp.concatenate(
        [wide[62:64], deep_w[63:64], depth_w[62:64], diag_w[63:64], jnp.zeros((2, WIDE), F32)], axis=0))
    down = (both_0, jnp.concatenate([two_0, nothing], axis=1), jnp.zeros((SLOT, WIDE), F32), jnp.concatenate(
        [wide[0:3], deep_w[0:1], depth_w[0:2], diag_w[0:2]], axis=0))
    for i in range(4):
        place = slice(i * SLOT, i * SLOT + (SLOT if i < 3 else 8))
        first_out[place] = jnp.where(even, up[i], down[i])
        second_out[place] = jnp.where(even, down[i], up[i])


def operate(field, half_depth, diag):
    east = pltpu.roll(field, WIDE - 1, 1)
    north = pltpu.roll(field, TALL - 1, 0)
    corner = pltpu.roll(north, WIDE - 1, 1)
    plus = half_depth * (corner - field)
    minus = half_depth * (east - north)
    return (diag * field - plus + pltpu.roll(minus, 1, 1)
            + pltpu.roll(pltpu.roll(plus, 1, 1) - minus, 1, 0)), plus, minus


def solver_kernel(weights, first, second, first_in, second_in, forcing, depth, diag,
                  part_one, part_two, zero_out, one_out, two_out, sums_out, full_one, full_two, strips, sems):
    inner = pl.ds(8, ROWS - 16)
    stores = [pltpu.make_async_copy(source.at[:, inner], target.at[:, inner], sems.at[4 + i])
              for i, (source, target) in enumerate(((part_one, full_one), (part_two, full_two)))]
    start_all(stores)
    own_up, own_down = by_side("by", first[...], second[...])
    above, beneath = by_side("by", first_in[...], second_in[...])
    level = iota((SLOT, WIDE), 0)
    mix, weight = (jnp.concatenate([weights[i:i + SLOT], weights[i:i + SLOT, :128]], axis=1) for i in (16, 16 + SLOT))
    level_f = level.astype(F32)

    def face(south, north, south_deep, north_deep):
        flow = south[2 * SLOT:3 * SLOT]
        wet = level_f < jnp.minimum(south_deep, north_deep)

        def flux(low, high):
            columns = low.shape[1]
            value = 0.5 * flow[:, :columns] * (low + high) - mix[:, :columns] * (high - low)
            return jnp.where(wet[:, :columns], value, 0.0)

        both = flux(south[:SLOT], north[:SLOT])
        two = flux(south[SLOT:2 * SLOT, :COLS], north[SLOT:2 * SLOT, :COLS])
        return jnp.sum(both * weight, axis=0, keepdims=True), both[:, :COLS] + 0.5 * two, two

    top, top_one, top_two = face(own_up, above, own_up[74:75], above[75:76])
    bottom, bottom_one, bottom_two = face(beneath, own_down, beneath[74:75], own_down[75:76])

    strip_row = iota((8, COLS), 0)
    for i, (source, flux, at, target) in enumerate((
            (part_one, bottom_one, 0, full_one), (part_two, bottom_two, 0, full_two),
            (part_one, -top_one, 7, full_one), (part_two, -top_two, 7, full_two))):
        start = 0 if at == 0 else ROWS - 8
        for k in range(LEV):
            strips[i, k] = source[k, start:start + 8] + jnp.where(strip_row == at, flux[k:k + 1], 0.0)
        stores.append(pltpu.make_async_copy(strips.at[i], target.at[:, pl.ds(start, 8)], sems.at[i]))
        stores[-1].start()

    def blank(count):
        return jnp.zeros((count, WIDE), F32)

    own_row = iota((ROWS, WIDE), 0)
    mine = forcing[...] + jnp.where(own_row == 0, bottom, jnp.where(own_row == ROWS - 1, -top, 0.0))
    field = jnp.concatenate([
        jnp.concatenate([blank(6), beneath[72:73], beneath[73:74] - bottom], axis=0), mine,
        jnp.concatenate([above[72:73] + top, above[73:75], blank(5)], axis=0)], axis=0)
    half_depth = 0.5 * jnp.concatenate([
        jnp.concatenate([blank(6), beneath[75:77]], axis=0), depth[...],
        jnp.concatenate([above[76:78], blank(6)], axis=0)], axis=0)
    diag_all = jnp.concatenate([
        jnp.concatenate([blank(7), beneath[77:78]], axis=0), diag[...],
        jnp.concatenate([above[78:80], blank(6)], axis=0)], axis=0)
    last = lax.axis_index("by") == lax.axis_size("by") - 1
    inside = iota((TALL, WIDE), 0) < jnp.where(last, ROWS + 8, TALL)

    image, _, _ = operate(field, half_depth, diag_all)
    image = jnp.where(inside, image, 0.0)
    twice, _, _ = operate(image, half_depth, diag_all)
    twice = jnp.where(inside, twice, 0.0)
    _, plus, minus = operate(twice, half_depth, diag_all)
    east = pltpu.roll(twice, WIDE - 1, 1)
    north = pltpu.roll(twice, TALL - 1, 0)
    corner = pltpu.roll(north, WIDE - 1, 1)
    energy = diag_all * twice * twice + plus * (corner - twice) + minus * (east - north)

    def own(value):
        return value[8:8 + ROWS, :COLS]

    v_0, v_1, v_2 = own(field), own(image), own(twice)
    zero_out[...], one_out[...], two_out[...] = v_0, v_1, v_2
    lane = iota((128, 128), 1)
    sums = jnp.zeros((128, 128), F32)
    for i, product in enumerate((v_0 * v_0, v_0 * v_1, v_1 * v_1, v_1 * v_2, v_2 * v_2, own(energy))):
        sums = jnp.where(lane == i, jnp.sum(product, keepdims=True), sums)
    sums_out[...] = sums
    wait_all(stores)


def surface_kernel(sums, zero, one, two, surface):
    total = jnp.sum(sums[...], axis=0, keepdims=True)
    m = [total[:, i:i + 1] for i in range(6)]
    a_0 = m[0] / m[1]
    rr_1 = m[0] - 2.0 * a_0 * m[1] + a_0 * a_0 * m[2]
    rar_1 = m[1] - 2.0 * a_0 * m[2] + a_0 * a_0 * m[3]
    b_1 = rr_1 / m[0]
    a_1 = rr_1 / (rar_1 - b_1 * rr_1 / a_0)
    grow = 1.0 + b_1
    p_1 = -(a_0 + a_1 * grow)
    p_2 = a_1 * a_0
    rr_2 = m[0] + p_1 * p_1 * m[2] + p_2 * p_2 * m[4] + 2.0 * (p_1 * m[1] + p_2 * m[2] + p_1 * p_2 * m[3])
    rar_2 = m[1] + p_1 * p_1 * m[3] + p_2 * p_2 * m[5] + 2.0 * (p_1 * m[2] + p_2 * m[3] + p_1 * p_2 * m[4])
    b_2 = rr_2 / rr_1
    a_2 = rr_2 / (rar_2 - b_2 * rr_2 / a_1)
    w_0 = a_0 + a_1 * grow + a_2 * (1.0 + b_2 * grow)
    w_1 = -a_1 * a_0 + a_2 * (p_1 - b_2 * a_0)
    w_2 = a_2 * p_2
    surface[...] = w_0 * zero[...] + w_1 * one[...] + w_2 * two[...]


def tracers_kernel(weights, one, two, east, north, deep_in, flux_left, flux_right, new_one, new_two,
                   east_deep, north_deep, edge):
    deep = deep_in[...].astype(jnp.int32)
    at_row = iota((ROWS, COLS), 0)
    east_deep[...] = jnp.minimum(deep, pltpu.roll(deep, COLS - 1, 1))
    north_deep[...] = jnp.where(at_row < ROWS - 1, jnp.minimum(deep, pltpu.roll(deep, ROWS - 1, 0)), 0)
    edge[...] = jnp.zeros(edge.shape, F32)
    row, lane = iota((CHUNK, COLS), 0), iota((CHUNK, 128), 1)

    @pl.loop(0, ROWS // CHUNK)
    def _(chunk):
        start = pl.multiple_of(chunk * CHUNK, CHUNK)
        part = pl.ds(start, CHUNK)
        here = deep_in[part].astype(jnp.int32)
        to_east, to_north = east_deep[part], north_deep[part]
        west_flux, east_flux = flux_left[part], flux_right[part]

        def level(k, falls):
            flow_e, flow_n = east[k, part].astype(F32), north[k, part].astype(F32)
            mix = 2.0 * weights[pl.ds(16 + k, 1)]
            below = jnp.minimum(k + 1, LEV - 1)
            wet, wet_east, wet_north = here > k, to_east > k, to_north > k
            east_own, east_next = jnp.where(wet_east, flow_e + mix, 0.0), jnp.where(wet_east, flow_e - mix, 0.0)
            north_own, north_next = jnp.where(wet_north, flow_n + mix, 0.0), jnp.where(wet_north, flow_n - mix, 0.0)
            fall_w = jnp.where(here > k + 1, weights[pl.ds(16 + 2 * SLOT + k, 1)], 0.0)
            kept_falls = []
            for i, (source, target) in enumerate(((one, new_one), (two, new_two))):
                c = source[k, part]
                e = east_own * c + east_next * pltpu.roll(c, COLS - 1, 1)
                seam = pltpu.roll(east_flux, 127 - k - i * LEV, 1)
                e = jnp.concatenate([e[:, :128], jnp.where(lane == 127, seam, e[:, 128:])], axis=1)
                e_west = pltpu.roll(e, 1, 1)
                seam = pltpu.roll(west_flux, lax.rem(256 - k - i * LEV, 128), 1)
                e_west = jnp.concatenate([jnp.where(lane == 0, seam, e_west[:, :128]), e_west[:, 128:]], axis=1)
                nxt = jnp.where(row == CHUNK - 1, source[k, pl.ds(start + CHUNK, 1)], pltpu.roll(c, CHUNK - 1, 0))
                n = north_own * c + north_next * nxt
                place = pl.ds(i * SLOT + k, 1)
                n_south = jnp.where(row == 0, edge[place], pltpu.roll(n, 1, 0))
                edge[place] = n[CHUNK - 1:]
                fall = fall_w * (source[below, part] - c)
                target[k, part] = jnp.where(
                    wet, c + (fall - falls[i]) - 0.5 * ((e - e_west) + (n - n_south)), 0.0)
                kept_falls.append(fall)
            return tuple(kept_falls)

        nothing = jnp.zeros((CHUNK, COLS), F32)
        lax.fori_loop(0, LEV, level, (nothing, nothing), unroll=TRACERS_UNROLL)

def cost(flops, moved):
    return pl.CostEstimate(flops=flops, bytes_accessed=moved, transcendentals=0)


def on_device(*arrays):
    (tracer_one, tracer_two, east_flow, north_flow, depth_levels, side_mix, vert_mix, thickness,
     corner_depth, diagonal) = (pltpu.with_memory_space_constraint(array, pltpu.HBM) for array in arrays)
    n_by, n_bx = lax.axis_size("by"), lax.axis_size("bx")
    cells = LEV * ROWS * COLS
    plane, wide, tile = shape(ROWS, COLS), shape(ROWS, WIDE), shape(ROWS, 128)
    block, taller = shape(LEV, ROWS, COLS), shape(LEV, ROWS + 8, COLS)
    half = jax.ShapeDtypeStruct((LEV, ROWS, COLS), jnp.bfloat16)
    column_message, row_message = shape(ROWS + SLOT, 128), shape(3 * SLOT + 8, WIDE)
    flat, flat_int = pltpu.VMEM((ROWS, COLS), F32), pltpu.VMEM((ROWS, COLS), jnp.int32)
    level_list = pltpu.SMEM((LEV,), F32)
    transfers = pltpu.SemaphoreType.DMA((4, ROWS // CHUNK))
    first, second, forcing, deep, depth, diag, edge_rows, weights, one, two, east, north = pl.pallas_call(
        forcing_kernel,
        out_shape=(column_message, column_message, plane, plane, plane, plane, shape(5 * SLOT, COLS),
                   shape(16 + 3 * SLOT, COLS), taller, taller, half, half),
        in_specs=[HBM] * 10,
        out_specs=(VMEM,) * 12,
        scratch_shapes=[level_list] * 3 + [flat_int, flat, flat] + [flat_int] * 2 + [flat] * 3
        + [pltpu.VMEM((ROWS, 128), F32)] * 2 + [transfers, pltpu.SemaphoreType.DMA((6,))],
        compiler_params=PARAMS, cost_estimate=cost(30 * cells, 12 * cells), name="forcing",
    )(side_mix, vert_mix, thickness, tracer_one, tracer_two, east_flow, north_flow, depth_levels, corner_depth, diagonal)
    first_in, second_in = swap_both(first, second, "bx", n_bx, True)
    row_first, row_second, forcing, depth, diag, flux_left, flux_right = pl.pallas_call(
        columns_kernel,
        out_shape=(row_message, row_message, wide, wide, wide, tile, tile),
        in_specs=[VMEM] * 10,
        out_specs=(VMEM,) * 7,
        compiler_params=PARAMS, cost_estimate=cost(10**6, 10**6), name="columns",
    )(weights, first, second, first_in, second_in, forcing, deep, depth, diag, edge_rows)
    row_first_in, row_second_in = swap_both(row_first, row_second, "by", n_by, False)
    part_one, part_two = pl.pallas_call(
        tracers_kernel,
        out_shape=(block, block),
        in_specs=[VMEM] * 8,
        out_specs=(VMEM,) * 2,
        scratch_shapes=[flat_int] * 2 + [pltpu.VMEM((2 * SLOT, COLS), F32)],
        compiler_params=PARAMS, cost_estimate=cost(60 * cells, 20 * cells), name="tracers",
    )(weights, one, two, east, north, deep, flux_left, flux_right)
    zero, one, two, sums, new_one, new_two = pl.pallas_call(
        solver_kernel,
        out_shape=(plane, plane, plane, shape(128, 128), block, block),
        in_specs=[VMEM] * 10,
        out_specs=(VMEM,) * 4 + (HBM,) * 2,
        scratch_shapes=[pltpu.VMEM((4, LEV, 8, COLS), F32), pltpu.SemaphoreType.DMA((6,))],
        compiler_params=PARAMS, cost_estimate=cost(4 * 10**6, 10**6), name="solver",
    )(weights, row_first, row_second, row_first_in, row_second_in, forcing, depth, diag, part_one, part_two)
    sums = lax.all_to_all(sums[:n_by * n_bx], ("by", "bx"), 0, 0, tiled=True)
    surface = pl.pallas_call(
        surface_kernel, out_shape=plane, in_specs=[VMEM] * 4, out_specs=VMEM,
        compiler_params=PARAMS, cost_estimate=cost(10**5, 10**5), name="surface",
    )(sums, zero, one, two)
    return new_one, new_two, surface


def solution(mesh):
    block, field = P(None, "by", "bx"), P("by", "bx")
    return jax.shard_map(
        on_device, mesh=mesh,
        in_specs=(block, block, block, block, field, P(), P(), P(), field, field),
        out_specs=(block, block, field), check_vma=False,
    )
```

```python
import jax
import jax.numpy as jnp
from jax import lax
from jax.experimental import pallas as pl
from jax.experimental.pallas import tpu as pltpu
from jax.sharding import PartitionSpec as P

LEV = 18
CHUNK = 16
SLOT = 24
ROWS, COLS = 64, 256
WIDE = COLS + 128
TALL = ROWS + 16
FORCING_UNROLL = 18
TRACERS_UNROLL = 6
F32 = jnp.float32
VMEM = pl.BlockSpec(memory_space=pltpu.VMEM)
SMEM = pl.BlockSpec(memory_space=pltpu.SMEM)
HBM = pl.BlockSpec(memory_space=pl.ANY)
PARAMS = pltpu.CompilerParams(vmem_limit_bytes=16 * 1024 * 1024)


def iota(shape, axis):
    return lax.broadcasted_iota(jnp.int32, shape, axis)


def shape(*dims):
    return jax.ShapeDtypeStruct(dims, F32)


def pairs(size, odd, wrap):
    swaps = []
    for low in range(1 if odd else 0, size, 2):
        high = low + 1
        if high == size and not wrap:
            continue
        swaps += [(low, high % size), (high % size, low)]
    return swaps


def swap_both(first, second, axis, size, wrap):
    return (
        lax.ppermute(first, axis, pairs(size, False, wrap)),
        lax.ppermute(second, axis, pairs(size, True, wrap)),
    )


def by_side(axis, first, second):
    even = lax.axis_index(axis) % 2 == 0
    return jnp.where(even, first, second), jnp.where(even, second, first)


def load_chunks(sources, targets, sems):
    def copy(array, chunk):
        part = pl.ds(pl.multiple_of(chunk * CHUNK, CHUNK), CHUNK)
        return pltpu.make_async_copy(sources[array].at[:, part], targets[array].at[:, part], sems.at[array, chunk])

    return copy


def start_all(copies):
    for copy in copies:
        copy.start()


def wait_all(copies):
    for copy in copies:
        copy.wait()


def forcing_kernel(side_hbm, vert_hbm, thick_hbm, one_hbm, two_hbm, east_hbm, north_hbm, levels_hbm, corner_hbm, diag_hbm,
                   first_out, second_out, forcing_out, deep_out, depth_out, diag_out, edge_rows, weights,
                   one, two, east, north, side, vert, thick, levels, corner, diag, east_deep, north_deep, east_sum, north_sum, column, right, left, sems, small):
    copy = load_chunks((one_hbm, two_hbm, east_hbm, north_hbm), (one, two, east, north), sems)
    chunks = ROWS // CHUNK
    pairs_of = ((levels_hbm, levels), (side_hbm, side), (vert_hbm, vert), (thick_hbm, thick), (corner_hbm, corner), (diag_hbm, diag))
    singles = [pltpu.make_async_copy(a, b, small.at[i]) for i, (a, b) in enumerate(pairs_of)]
    start_all(singles[:4])
    for chunk in range(chunks):
        start_all(copy(array, chunk) for array in range(4))
    start_all(singles[4:])
    for array in (one, two):
        array[:, ROWS:] = jnp.zeros((LEV, 8, COLS), F32)
    wait_all(singles[:4])
    deep = levels[...]
    at_row, at_col = iota((ROWS, COLS), 0), iota((ROWS, COLS), 1)
    east_deep[...] = jnp.where(at_col < COLS - 1, jnp.minimum(deep, pltpu.roll(deep, COLS - 1, 1)), 0)
    north_deep[...] = jnp.where(at_row < ROWS - 1, jnp.minimum(deep, pltpu.roll(deep, ROWS - 1, 0)), 0)
    edge_rows[...] = jnp.zeros(edge_rows.shape, F32)
    row, lane = iota((CHUNK, COLS), 0), iota((CHUNK, 128), 1)
    wait_all(copy(array, 0) for array in range(4))

    @pl.loop(0, chunks)
    def _(chunk):
        @pl.when(chunk + 1 < chunks)
        def _():
            wait_all(copy(array, chunk + 1) for array in range(4))

        start = pl.multiple_of(chunk * CHUNK, CHUNK)
        part = pl.ds(start, CHUNK)
        here, to_east, to_north = levels[part], east_deep[part], north_deep[part]

        def level(k, carry):
            e_sum, n_sum, total, to_right, to_left = carry
            c_one, c_two = one[k, part], two[k, part]
            flow_e, flow_n = east[k, part].astype(F32), north[k, part].astype(F32)
            both = c_one - 0.5 * c_two
            beyond = one[k, pl.ds(start + CHUNK, 1)] - 0.5 * two[k, pl.ds(start + CHUNK, 1)]
            weight, mix = thick[k], 2.0 * side[k]
            below, above = jnp.minimum(k + 1, LEV - 1), jnp.maximum(k - 1, 0)
            fall = (weight - thick[below]) * vert[k]
            fall_above = (thick[above] - weight) * vert[above]
            total = total + both * jnp.where(
                here > k + 1, weight + fall_above - fall, jnp.where(here > k, weight + fall_above, 0.0))
            both, beyond = (0.5 * weight) * both, (0.5 * weight) * beyond
            nxt = pltpu.roll(both, COLS - 1, 1)
            e_sum = e_sum + jnp.where(to_east > k, flow_e * (both + nxt) - mix * (nxt - both), 0.0)
            nxt = jnp.where(row == CHUNK - 1, beyond, pltpu.roll(both, CHUNK - 1, 0))
            n_sum = n_sum + jnp.where(to_north > k, flow_n * (both + nxt) - mix * (nxt - both), 0.0)
            to_right = jnp.where(lane == k, c_one[:, COLS - 1:], to_right)
            to_right = jnp.where(lane == k + LEV, c_two[:, COLS - 1:], to_right)
            to_right = jnp.where((lane == k + 2 * LEV) | (lane == k + 3 * LEV), flow_e[:, COLS - 1:], to_right)
            to_left = jnp.where(lane == k + 64, c_one[:, :1], to_left)
            to_left = jnp.where(lane == k + 64 + LEV, c_two[:, :1], to_left)
            return e_sum, n_sum, total, to_right, to_left

        flat, tile = jnp.zeros((CHUNK, COLS), F32), jnp.zeros((CHUNK, 128), F32)
        result = lax.fori_loop(0, LEV, level, (flat, flat, flat, tile, tile), unroll=FORCING_UNROLL)
        for target, value in zip((east_sum, north_sum, column, right, left), result):
            target[part] = value

    for k in range(LEV):
        rows = (one[k, 0:1], two[k, 0:1], one[k, ROWS - 1:ROWS], two[k, ROWS - 1:ROWS],
                north[k, ROWS - 16:ROWS].astype(F32)[15:])
        for i, value in enumerate(rows):
            edge_rows[i * SLOT + k:i * SLOT + k + 1] = value

    at, level = iota((8, COLS), 1), iota((SLOT, COLS), 0)
    lane_mix = lane_weight = jnp.zeros((8, COLS), F32)
    row_mix = row_weight = row_vert = jnp.zeros((SLOT, COLS), F32)
    for k in range(LEV):
        lane_mix = jnp.where((at == k) | (at == k + LEV), side[k], lane_mix)
        lane_weight = jnp.where(at == k, thick[k], jnp.where(at == k + LEV, -0.5 * thick[k], lane_weight))
        row_mix = jnp.where(level == k, side[k], row_mix)
        row_weight = jnp.where(level == k, thick[k], row_weight)
        row_vert = jnp.where(level == k, vert[k], row_vert)
    weights[...] = jnp.concatenate([lane_mix, lane_weight, row_mix, row_weight, row_vert], axis=0)
    e_sum, n_sum = east_sum[...], north_sum[...]
    forcing = column[...] - (e_sum - pltpu.roll(e_sum, 1, 1)) - (n_sum - pltpu.roll(n_sum, 1, 0))
    forcing_out[...] = forcing
    wait_all(singles[4:])
    depth = jnp.where(deep > 0, corner[...], 0.0)
    fields = (forcing, depth, diag[...], deep.astype(F32))
    deep_out[...], depth_out[...], diag_out[...] = fields[3], fields[1], fields[2]
    to_right, to_left = right[...], left[...]
    lane = iota((ROWS, 128), 1)
    for i, field in enumerate(fields):
        tile = field[:, COLS - 128:]
        tile = pltpu.roll(tile, 128 - 2 * i, 1) if i else tile
        to_right = jnp.where((lane >= 126 - 2 * i) & (lane < 128 - 2 * i), tile, to_right)
        tile = field[:, :128]
        tile = pltpu.roll(tile, 3 * i, 1) if i else tile
        to_left = jnp.where((lane >= 3 * i) & (lane < 3 * i + 3), tile, to_left)
    rows_0 = edge_rows[0:SLOT] - 0.5 * edge_rows[SLOT:2 * SLOT]
    rows_1 = edge_rows[2 * SLOT:3 * SLOT] - 0.5 * edge_rows[3 * SLOT:4 * SLOT]
    rows_2 = edge_rows[4 * SLOT:5 * SLOT]
    lane = iota((SLOT, 128), 1)
    corner_right = corner_left = jnp.zeros((SLOT, 128), F32)
    for i, rows in enumerate((rows_0, rows_1, rows_2)):
        tile = rows[:, COLS - 128:]
        tile = pltpu.roll(tile, 128 - 2 * i, 1) if i else tile
        corner_right = jnp.where((lane >= 126 - 2 * i) & (lane < 128 - 2 * i), tile, corner_right)
        tile = rows[:, :128]
        tile = pltpu.roll(tile, 3 * i, 1) if i else tile
        corner_left = jnp.where((lane >= 3 * i) & (lane < 3 * i + 3), tile, corner_left)
    even = lax.axis_index("bx") % 2 == 0
    first_out[:ROWS] = jnp.where(even, to_right, to_left)
    second_out[:ROWS] = jnp.where(even, to_left, to_right)
    first_out[ROWS:] = jnp.where(even, corner_right, corner_left)
    second_out[ROWS:] = jnp.where(even, corner_left, corner_right)


def lane_tile(from_right, from_left, i):
    lane = iota(from_right.shape, 1)
    if i:
        from_right, from_left = pltpu.roll(from_right, 128 - 3 * i, 1), pltpu.roll(from_left, 2 * i, 1)
    return jnp.where(lane < 3, from_right, jnp.where(lane >= 126, from_left, 0.0))


def columns_kernel(weights, first, second, first_in, second_in, forcing, deep_in, depth_in, diag, edge_rows, after,
                   first_out, second_out, forcing_wide, depth_wide, diag_wide, flux_left, flux_right):
    own_right, own_left = by_side("bx", first[...], second[...])
    from_right, from_left = by_side("bx", first_in[...], second_in[...])
    deep_f, depth = deep_in[...], depth_in[...]
    lane = iota((ROWS, 128), 1)
    at = iota((8, 128), 1)
    mix, weight = weights[0:1, :128], weights[8:9, :128]
    of_lane = jnp.where(at < LEV, at, jnp.where(at < 2 * LEV, at - LEV, 100))[:1].astype(F32)

    def face(west, east, flow, west_deep, east_deep):
        flux = 0.5 * flow * (west + east) - mix * (east - west)
        flux = jnp.where(of_lane < jnp.minimum(west_deep, east_deep), flux, 0.0)
        return flux, jnp.sum(flux * weight, axis=1, keepdims=True)

    own, seen = own_left[:ROWS], from_left[:ROWS]
    flux, west_sum = face(seen, pltpu.roll(own, 64, 1), pltpu.roll(seen, 128 - 2 * LEV, 1), seen[:, 121:122], deep_f[:, :1])
    flux_left[...] = flux
    own, seen = own_right[:ROWS], from_right[:ROWS]
    flux, east_sum = face(own, pltpu.roll(seen, 64, 1), pltpu.roll(own, 128 - 2 * LEV, 1), deep_f[:, COLS - 1:], seen[:, 9:10])
    flux_right[...] = flux

    mine = forcing[...]
    tiles = (
        mine[:, :128] + jnp.where(lane == 0, west_sum, 0.0),
        mine[:, 128:] - jnp.where(lane == 127, east_sum, 0.0),
        lane_tile(from_right[:ROWS], from_left[:ROWS], 0)
        + jnp.where(lane == 0, east_sum, jnp.where(lane == 127, -west_sum, 0.0)),
    )
    wide = jnp.concatenate(tiles, axis=1)
    forcing_wide[...] = wide
    depth_w = jnp.concatenate([depth, lane_tile(from_right[:ROWS], from_left[:ROWS], 1)], axis=1)
    diag_w = jnp.concatenate([diag[...], lane_tile(from_right[:ROWS], from_left[:ROWS], 2)], axis=1)
    deep_w = jnp.concatenate([deep_f, lane_tile(from_right[:ROWS], from_left[:ROWS], 3)], axis=1)
    depth_wide[...] = depth_w
    diag_wide[...] = diag_w

    def rows(value, i):
        return jnp.concatenate([value, lane_tile(from_right[ROWS:], from_left[ROWS:], i)], axis=1)

    nothing = jnp.zeros((SLOT, 128), F32)
    two_0, two_1 = edge_rows[SLOT:2 * SLOT], edge_rows[3 * SLOT:4 * SLOT]
    both_0 = rows(edge_rows[0:SLOT] - 0.5 * two_0, 0)
    both_1 = rows(edge_rows[2 * SLOT:3 * SLOT] - 0.5 * two_1, 1)
    north_1 = rows(edge_rows[4 * SLOT:5 * SLOT], 2)
    even = lax.axis_index("by") % 2 == 0
    up = (both_1, jnp.concatenate([two_1, nothing], axis=1), north_1, jnp.concatenate(
        [wide[62:64], deep_w[63:64], depth_w[62:64], diag_w[63:64], jnp.zeros((2, WIDE), F32)], axis=0))
    down = (both_0, jnp.concatenate([two_0, nothing], axis=1), jnp.zeros((SLOT, WIDE), F32), jnp.concatenate(
        [wide[0:3], deep_w[0:1], depth_w[0:2], diag_w[0:2]], axis=0))
    for i in range(4):
        place = slice(i * SLOT, i * SLOT + (SLOT if i < 3 else 8))
        first_out[place] = jnp.where(even, up[i], down[i])
        second_out[place] = jnp.where(even, down[i], up[i])


def operate(field, half_depth, diag):
    east = pltpu.roll(field, WIDE - 1, 1)
    north = pltpu.roll(field, TALL - 1, 0)
    corner = pltpu.roll(north, WIDE - 1, 1)
    plus = half_depth * (corner - field)
    minus = half_depth * (east - north)
    return (diag * field - plus + pltpu.roll(minus, 1, 1)
            + pltpu.roll(pltpu.roll(plus, 1, 1) - minus, 1, 0)), plus, minus


def solver_kernel(weights, first, second, first_in, second_in, forcing, depth, diag, after,
                  zero_out, one_out, two_out, sums_out, flux_rows):
    own_up, own_down = by_side("by", first[...], second[...])
    above, beneath = by_side("by", first_in[...], second_in[...])
    level = iota((SLOT, WIDE), 0)
    mix, weight = (jnp.concatenate([weights[i:i + SLOT], weights[i:i + SLOT, :128]], axis=1) for i in (16, 16 + SLOT))
    level_f = level.astype(F32)

    def face(south, north, south_deep, north_deep):
        flow = south[2 * SLOT:3 * SLOT]
        wet = level_f < jnp.minimum(south_deep, north_deep)

        def flux(low, high):
            columns = low.shape[1]
            value = 0.5 * flow[:, :columns] * (low + high) - mix[:, :columns] * (high - low)
            return jnp.where(wet[:, :columns], value, 0.0)

        both = flux(south[:SLOT], north[:SLOT])
        two = flux(south[SLOT:2 * SLOT, :COLS], north[SLOT:2 * SLOT, :COLS])
        return jnp.sum(both * weight, axis=0, keepdims=True), both[:, :COLS] + 0.5 * two, two

    top, top_one, top_two = face(own_up, above, own_up[74:75], above[75:76])
    bottom, bottom_one, bottom_two = face(beneath, own_down, beneath[74:75], own_down[75:76])

    for i, flux in enumerate((bottom_one, bottom_two, top_one, top_two)):
        flux_rows[i * SLOT:(i + 1) * SLOT] = flux

    def blank(count):
        return jnp.zeros((count, WIDE), F32)

    own_row = iota((ROWS, WIDE), 0)
    mine = forcing[...] + jnp.where(own_row == 0, bottom, jnp.where(own_row == ROWS - 1, -top, 0.0))
    field = jnp.concatenate([
        jnp.concatenate([blank(6), beneath[72:73], beneath[73:74] - bottom], axis=0), mine,
        jnp.concatenate([above[72:73] + top, above[73:75], blank(5)], axis=0)], axis=0)
    half_depth = 0.5 * jnp.concatenate([
        jnp.concatenate([blank(6), beneath[75:77]], axis=0), depth[...],
        jnp.concatenate([above[76:78], blank(6)], axis=0)], axis=0)
    diag_all = jnp.concatenate([
        jnp.concatenate([blank(7), beneath[77:78]], axis=0), diag[...],
        jnp.concatenate([above[78:80], blank(6)], axis=0)], axis=0)
    last = lax.axis_index("by") == lax.axis_size("by") - 1
    inside = iota((TALL, WIDE), 0) < jnp.where(last, ROWS + 8, TALL)

    image, _, _ = operate(field, half_depth, diag_all)
    image = jnp.where(inside, image, 0.0)
    twice, _, _ = operate(image, half_depth, diag_all)
    twice = jnp.where(inside, twice, 0.0)
    _, plus, minus = operate(twice, half_depth, diag_all)
    east = pltpu.roll(twice, WIDE - 1, 1)
    north = pltpu.roll(twice, TALL - 1, 0)
    corner = pltpu.roll(north, WIDE - 1, 1)
    energy = diag_all * twice * twice + plus * (corner - twice) + minus * (east - north)

    def own(value):
        return value[8:8 + ROWS, :COLS]

    v_0, v_1, v_2 = own(field), own(image), own(twice)
    zero_out[...], one_out[...], two_out[...] = v_0, v_1, v_2
    lane = iota((128, 128), 1)
    sums = jnp.zeros((128, 128), F32)
    for i, product in enumerate((v_0 * v_0, v_0 * v_1, v_1 * v_1, v_1 * v_2, v_2 * v_2, own(energy))):
        sums = jnp.where(lane == i, jnp.sum(product, keepdims=True), sums)
    sums_out[...] = sums


def surface_kernel(sums, zero, one, two, flux_rows, new_one, new_two, inner_one, inner_two,
                   surface_out, full_one, full_two, surface, strips, sems):
    row = iota((8, COLS), 0)
    stores = []
    for i, (source, target) in enumerate(((new_one, full_one), (new_two, full_two))):
        part = pl.ds(ROWS - CHUNK, CHUNK - 8)
        stores.append(pltpu.make_async_copy(source.at[:, part], target.at[:, part], sems.at[4 + i]))
        stores[-1].start()
    for i, (source, at, sign, target) in enumerate((
            (new_one, 0, 1.0, full_one), (new_two, 0, 1.0, full_two),
            (new_one, 7, -1.0, full_one), (new_two, 7, -1.0, full_two))):
        start = 0 if at == 0 else ROWS - 8
        for k in range(LEV):
            place = i * SLOT + k
            strips[i, k] = source[k, start:start + 8] + jnp.where(row == at, sign * flux_rows[place:place + 1], 0.0)
        stores.append(pltpu.make_async_copy(strips.at[i], target.at[:, pl.ds(start, 8)], sems.at[i]))
        stores[-1].start()
    total = jnp.sum(sums[...], axis=0, keepdims=True)
    m = [total[:, i:i + 1] for i in range(6)]
    a_0 = m[0] / m[1]
    rr_1 = m[0] - 2.0 * a_0 * m[1] + a_0 * a_0 * m[2]
    rar_1 = m[1] - 2.0 * a_0 * m[2] + a_0 * a_0 * m[3]
    b_1 = rr_1 / m[0]
    a_1 = rr_1 / (rar_1 - b_1 * rr_1 / a_0)
    grow = 1.0 + b_1
    p_1 = -(a_0 + a_1 * grow)
    p_2 = a_1 * a_0
    rr_2 = m[0] + p_1 * p_1 * m[2] + p_2 * p_2 * m[4] + 2.0 * (p_1 * m[1] + p_2 * m[2] + p_1 * p_2 * m[3])
    rar_2 = m[1] + p_1 * p_1 * m[3] + p_2 * p_2 * m[5] + 2.0 * (p_1 * m[2] + p_2 * m[3] + p_1 * p_2 * m[4])
    b_2 = rr_2 / rr_1
    a_2 = rr_2 / (rar_2 - b_2 * rr_2 / a_1)
    w_0 = a_0 + a_1 * grow + a_2 * (1.0 + b_2 * grow)
    w_1 = -a_1 * a_0 + a_2 * (p_1 - b_2 * a_0)
    w_2 = a_2 * p_2
    surface[...] = w_0 * zero[...] + w_1 * one[...] + w_2 * two[...]
    stores.append(pltpu.make_async_copy(surface, surface_out, sems.at[6]))
    stores[-1].start()
    wait_all(stores)


def tracers_kernel(weights, one, two, east, north, deep_in, part_one, part_two, east_deep, north_deep, edge):
    deep = deep_in[...].astype(jnp.int32)
    at_row, at_col = iota((ROWS, COLS), 0), iota((ROWS, COLS), 1)
    east_deep[...] = jnp.where(at_col < COLS - 1, jnp.minimum(deep, pltpu.roll(deep, COLS - 1, 1)), 0)
    north_deep[...] = jnp.where(at_row < ROWS - 1, jnp.minimum(deep, pltpu.roll(deep, ROWS - 1, 0)), 0)
    edge[...] = jnp.zeros(edge.shape, F32)
    row = iota((CHUNK, COLS), 0)

    @pl.loop(0, ROWS // CHUNK)
    def _(chunk):
        start = pl.multiple_of(chunk * CHUNK, CHUNK)
        part = pl.ds(start, CHUNK)
        here, to_east, to_north = deep_in[part].astype(jnp.int32), east_deep[part], north_deep[part]

        def level(k, falls):
            flow_e, flow_n = east[k, part].astype(F32), north[k, part].astype(F32)
            mix = 2.0 * weights[pl.ds(16 + k, 1)]
            below = jnp.minimum(k + 1, LEV - 1)
            wet, wet_east, wet_north = here > k, to_east > k, to_north > k
            east_own, east_next = jnp.where(wet_east, flow_e + mix, 0.0), jnp.where(wet_east, flow_e - mix, 0.0)
            north_own, north_next = jnp.where(wet_north, flow_n + mix, 0.0), jnp.where(wet_north, flow_n - mix, 0.0)
            fall_w = jnp.where(here > k + 1, weights[pl.ds(16 + 2 * SLOT + k, 1)], 0.0)
            kept_falls = []
            for i, (source, target) in enumerate(((one, part_one), (two, part_two))):
                c = source[k, part]
                e = east_own * c + east_next * pltpu.roll(c, COLS - 1, 1)
                nxt = jnp.where(row == CHUNK - 1, source[k, pl.ds(start + CHUNK, 1)], pltpu.roll(c, CHUNK - 1, 0))
                n = north_own * c + north_next * nxt
                place = pl.ds(i * SLOT + k, 1)
                n_south = jnp.where(row == 0, edge[place], pltpu.roll(n, 1, 0))
                edge[place] = n[CHUNK - 1:]
                fall = fall_w * (source[below, part] - c)
                target[k, part] = jnp.where(
                    wet, c + (fall - falls[i]) - 0.5 * ((e - pltpu.roll(e, 1, 1)) + (n - n_south)), 0.0)
                kept_falls.append(fall)
            return tuple(kept_falls)

        nothing = jnp.zeros((CHUNK, COLS), F32)
        lax.fori_loop(0, LEV, level, (nothing, nothing), unroll=TRACERS_UNROLL)


def edges_kernel(flux_left, flux_right, part_one, part_two, one_out, two_out, new_one, new_two, sems):
    kept = ((8, CHUNK - 8), (CHUNK, CHUNK), (2 * CHUNK, CHUNK))
    stores = []
    lane = iota((CHUNK, 128), 1)
    for chunk in range(ROWS // CHUNK):
        part = pl.ds(chunk * CHUNK, CHUNK)
        west_flux, east_flux = flux_left[part], flux_right[part]
        for i, (source, target, out) in enumerate(((part_one, new_one, one_out), (part_two, new_two, two_out))):
            for k in range(LEV):
                at = k + i * LEV
                seam = pltpu.roll(west_flux, 128 - at, 1) if at else west_flux
                target[k, part, :128] = source[k, part, :128] + jnp.where(lane == 0, seam, 0.0)
                seam = pltpu.roll(east_flux, 127 - at, 1)
                target[k, part, 128:] = source[k, part, 128:] - jnp.where(lane == 127, seam, 0.0)
            if chunk < len(kept):
                place = pl.ds(*kept[chunk])
                stores.append(pltpu.make_async_copy(target.at[:, place], out.at[:, place], sems.at[i, chunk]))
                stores[-1].start()
    wait_all(stores)


def cost(flops, moved):
    return pl.CostEstimate(flops=flops, bytes_accessed=moved, transcendentals=0)


def on_device(*arrays):
    (tracer_one, tracer_two, east_flow, north_flow, depth_levels, side_mix, vert_mix, thickness,
     corner_depth, diagonal) = (pltpu.with_memory_space_constraint(array, pltpu.HBM) for array in arrays)
    n_by, n_bx = lax.axis_size("by"), lax.axis_size("bx")
    cells = LEV * ROWS * COLS
    plane, wide, tile = shape(ROWS, COLS), shape(ROWS, WIDE), shape(ROWS, 128)
    block, taller = shape(LEV, ROWS, COLS), shape(LEV, ROWS + 8, COLS)
    half = jax.ShapeDtypeStruct((LEV, ROWS, COLS), jnp.bfloat16)
    column_message, row_message = shape(ROWS + SLOT, 128), shape(3 * SLOT + 8, WIDE)
    flat, flat_int = pltpu.VMEM((ROWS, COLS), F32), pltpu.VMEM((ROWS, COLS), jnp.int32)
    level_list = pltpu.SMEM((LEV,), F32)
    transfers = pltpu.SemaphoreType.DMA((4, ROWS // CHUNK))
    first, second, forcing, deep, depth, diag, edge_rows, weights, one, two, east, north = pl.pallas_call(
        forcing_kernel,
        out_shape=(column_message, column_message, plane, plane, plane, plane, shape(5 * SLOT, COLS),
                   shape(16 + 3 * SLOT, COLS), taller, taller, half, half),
        in_specs=[HBM] * 10,
        out_specs=(VMEM,) * 12,
        scratch_shapes=[level_list] * 3 + [flat_int, flat, flat] + [flat_int] * 2 + [flat] * 3
        + [pltpu.VMEM((ROWS, 128), F32)] * 2 + [transfers, pltpu.SemaphoreType.DMA((6,))],
        compiler_params=PARAMS, cost_estimate=cost(30 * cells, 12 * cells), name="forcing",
    )(side_mix, vert_mix, thickness, tracer_one, tracer_two, east_flow, north_flow, depth_levels, corner_depth, diagonal)
    part_one, part_two = pl.pallas_call(
        tracers_kernel,
        out_shape=(block, block),
        in_specs=[VMEM] * 6,
        out_specs=(VMEM,) * 2,
        scratch_shapes=[flat_int] * 2 + [pltpu.VMEM((2 * SLOT, COLS), F32)],
        compiler_params=PARAMS, cost_estimate=cost(60 * cells, 20 * cells), name="tracers",
    )(weights, one, two, east, north, deep)
    first_in, second_in = swap_both(first, second, "bx", n_bx, True)
    row_first, row_second, forcing, depth, diag, flux_left, flux_right = pl.pallas_call(
        columns_kernel,
        out_shape=(row_message, row_message, wide, wide, wide, tile, tile),
        in_specs=[VMEM] * 10 + [HBM],
        out_specs=(VMEM,) * 7,
        compiler_params=PARAMS, cost_estimate=cost(10**6, 10**6), name="columns",
    )(weights, first, second, first_in, second_in, forcing, deep, depth, diag, edge_rows, part_one)
    row_first_in, row_second_in = swap_both(row_first, row_second, "by", n_by, False)
    inner_one, inner_two, edge_one, edge_two = pl.pallas_call(
        edges_kernel,
        out_shape=(block, block, block, block),
        in_specs=[VMEM] * 4,
        out_specs=(HBM,) * 2 + (VMEM,) * 2,
        scratch_shapes=[pltpu.SemaphoreType.DMA((2, ROWS // CHUNK))],
        compiler_params=PARAMS, cost_estimate=cost(10 * cells, 10 * cells), name="edges",
    )(flux_left, flux_right, part_one, part_two)
    v_0, v_1, v_2, sums, flux_rows = pl.pallas_call(
        solver_kernel,
        out_shape=(plane, plane, plane, shape(128, 128), shape(4 * SLOT, COLS)),
        in_specs=[VMEM] * 8 + [HBM],
        out_specs=(VMEM,) * 5,
        compiler_params=PARAMS, cost_estimate=cost(4 * 10**6, 10**6), name="solver",
    )(weights, row_first, row_second, row_first_in, row_second_in, forcing, depth, diag, edge_one)
    sums = lax.all_to_all(sums[:n_by * n_bx], ("by", "bx"), 0, 0, tiled=True)
    surface, new_one, new_two = pl.pallas_call(
        surface_kernel,
        out_shape=(plane, block, block),
        in_specs=[VMEM] * 7 + [HBM] * 2,
        out_specs=(HBM,) * 3,
        input_output_aliases={7: 1, 8: 2},
        scratch_shapes=[flat, pltpu.VMEM((4, LEV, 8, COLS), F32), pltpu.SemaphoreType.DMA((7,))],
        compiler_params=PARAMS, cost_estimate=cost(10**5, 10**5), name="surface",
    )(sums, v_0, v_1, v_2, flux_rows, edge_one, edge_two, inner_one, inner_two)
    return new_one, new_two, surface


def solution(mesh):
    block, field = P(None, "by", "bx"), P("by", "bx")
    return jax.shard_map(
        on_device, mesh=mesh,
        in_specs=(block, block, block, block, field, P(), P(), P(), field, field),
        out_specs=(block, block, field), check_vma=False,
    )
```

```python
import jax
import jax.numpy as jnp
from jax import lax
from jax.experimental import pallas as pl
from jax.experimental.pallas import tpu as pltpu
from jax.sharding import PartitionSpec as P

LEV = 18
CHUNK = 16
SLOT = 24
ROWS, COLS = 64, 256
WIDE = COLS + 128
TALL = ROWS + 16
FORCING_UNROLL = 18
TRACERS_UNROLL = 6
F32 = jnp.float32
VMEM = pl.BlockSpec(memory_space=pltpu.VMEM)
SMEM = pl.BlockSpec(memory_space=pltpu.SMEM)
HBM = pl.BlockSpec(memory_space=pl.ANY)
PARAMS = pltpu.CompilerParams(vmem_limit_bytes=16 * 1024 * 1024)


def iota(shape, axis):
    return lax.broadcasted_iota(jnp.int32, shape, axis)


def shape(*dims):
    return jax.ShapeDtypeStruct(dims, F32)


def pairs(size, odd, wrap):
    swaps = []
    for low in range(1 if odd else 0, size, 2):
        high = low + 1
        if high == size and not wrap:
            continue
        swaps += [(low, high % size), (high % size, low)]
    return swaps


def swap_both(first, second, axis, size, wrap):
    return (
        lax.ppermute(first, axis, pairs(size, False, wrap)),
        lax.ppermute(second, axis, pairs(size, True, wrap)),
    )


def by_side(axis, first, second):
    even = lax.axis_index(axis) % 2 == 0
    return jnp.where(even, first, second), jnp.where(even, second, first)


def load_chunks(sources, targets, sems):
    def copy(array, chunk):
        part = pl.ds(pl.multiple_of(chunk * CHUNK, CHUNK), CHUNK)
        return pltpu.make_async_copy(sources[array].at[:, part], targets[array].at[:, part], sems.at[array, chunk])

    return copy


def start_all(copies):
    for copy in copies:
        copy.start()


def wait_all(copies):
    for copy in copies:
        copy.wait()


def forcing_kernel(side_hbm, vert_hbm, thick_hbm, one_hbm, two_hbm, east_hbm, north_hbm, levels_hbm, corner_hbm, diag_hbm,
                   first_out, second_out, forcing_out, deep_out, depth_out, diag_out, edge_rows, weights,
                   one, two, east, north, side, vert, thick, levels, corner, diag, east_deep, north_deep, east_sum, north_sum, column, right, left, sems, small):
    copy = load_chunks((one_hbm, two_hbm, east_hbm, north_hbm), (one, two, east, north), sems)
    chunks = ROWS // CHUNK
    pairs_of = ((levels_hbm, levels), (side_hbm, side), (vert_hbm, vert), (thick_hbm, thick), (corner_hbm, corner), (diag_hbm, diag))
    singles = [pltpu.make_async_copy(a, b, small.at[i]) for i, (a, b) in enumerate(pairs_of)]
    start_all(singles[:4])
    for chunk in range(chunks):
        start_all(copy(array, chunk) for array in range(4))
    start_all(singles[4:])
    for array in (one, two):
        array[:, ROWS:] = jnp.zeros((LEV, 8, COLS), F32)
    wait_all(singles[:4])
    deep = levels[...]
    at_row, at_col = iota((ROWS, COLS), 0), iota((ROWS, COLS), 1)
    east_deep[...] = jnp.where(at_col < COLS - 1, jnp.minimum(deep, pltpu.roll(deep, COLS - 1, 1)), 0)
    north_deep[...] = jnp.where(at_row < ROWS - 1, jnp.minimum(deep, pltpu.roll(deep, ROWS - 1, 0)), 0)
    edge_rows[...] = jnp.zeros(edge_rows.shape, F32)
    row, lane = iota((CHUNK, COLS), 0), iota((CHUNK, 128), 1)
    wait_all(copy(array, 0) for array in range(4))

    @pl.loop(0, chunks)
    def _(chunk):
        @pl.when(chunk + 1 < chunks)
        def _():
            wait_all(copy(array, chunk + 1) for array in range(4))

        start = pl.multiple_of(chunk * CHUNK, CHUNK)
        part = pl.ds(start, CHUNK)
        here, to_east, to_north = levels[part], east_deep[part], north_deep[part]

        def level(k, carry):
            e_sum, n_sum, total, to_right, to_left = carry
            c_one, c_two = one[k, part], two[k, part]
            flow_e, flow_n = east[k, part].astype(F32), north[k, part].astype(F32)
            both = c_one - 0.5 * c_two
            beyond = one[k, pl.ds(start + CHUNK, 1)] - 0.5 * two[k, pl.ds(start + CHUNK, 1)]
            weight, mix = thick[k], 2.0 * side[k]
            below, above = jnp.minimum(k + 1, LEV - 1), jnp.maximum(k - 1, 0)
            fall = (weight - thick[below]) * vert[k]
            fall_above = (thick[above] - weight) * vert[above]
            total = total + both * jnp.where(
                here > k + 1, weight + fall_above - fall, jnp.where(here > k, weight + fall_above, 0.0))
            both, beyond = (0.5 * weight) * both, (0.5 * weight) * beyond
            nxt = pltpu.roll(both, COLS - 1, 1)
            e_sum = e_sum + jnp.where(to_east > k, flow_e * (both + nxt) - mix * (nxt - both), 0.0)
            nxt = jnp.where(row == CHUNK - 1, beyond, pltpu.roll(both, CHUNK - 1, 0))
            n_sum = n_sum + jnp.where(to_north > k, flow_n * (both + nxt) - mix * (nxt - both), 0.0)
            for i, value in enumerate((c_one, c_two, flow_e)):
                at = k + i * LEV
                to_right = jnp.where(lane == at, pltpu.roll(value[:, COLS - 128:], at + 1, 1), to_right)
            for i, value in enumerate((c_one, c_two)):
                at = k + i * LEV + 64
                to_left = jnp.where(lane == at, pltpu.roll(value[:, :128], at, 1), to_left)
            return e_sum, n_sum, total, to_right, to_left

        flat, tile = jnp.zeros((CHUNK, COLS), F32), jnp.zeros((CHUNK, 128), F32)
        result = lax.fori_loop(0, LEV, level, (flat, flat, flat, tile, tile), unroll=FORCING_UNROLL)
        for target, value in zip((east_sum, north_sum, column, right, left), result):
            target[part] = value

    for k in range(LEV):
        rows = (one[k, 0:1], two[k, 0:1], one[k, ROWS - 1:ROWS], two[k, ROWS - 1:ROWS],
                north[k, ROWS - 16:ROWS].astype(F32)[15:])
        for i, value in enumerate(rows):
            edge_rows[i * SLOT + k:i * SLOT + k + 1] = value

    at, level = iota((8, COLS), 1), iota((SLOT, COLS), 0)
    lane_mix = lane_weight = jnp.zeros((8, COLS), F32)
    row_mix = row_weight = row_vert = jnp.zeros((SLOT, COLS), F32)
    for k in range(LEV):
        lane_mix = jnp.where((at == k) | (at == k + LEV), side[k], lane_mix)
        lane_weight = jnp.where(at == k, thick[k], jnp.where(at == k + LEV, -0.5 * thick[k], lane_weight))
        row_mix = jnp.where(level == k, side[k], row_mix)
        row_weight = jnp.where(level == k, thick[k], row_weight)
        row_vert = jnp.where(level == k, vert[k], row_vert)
    weights[...] = jnp.concatenate([lane_mix, lane_weight, row_mix, row_weight, row_vert], axis=0)
    e_sum, n_sum = east_sum[...], north_sum[...]
    forcing = column[...] - (e_sum - pltpu.roll(e_sum, 1, 1)) - (n_sum - pltpu.roll(n_sum, 1, 0))
    forcing_out[...] = forcing
    wait_all(singles[4:])
    depth = jnp.where(deep > 0, corner[...], 0.0)
    fields = (forcing, depth, diag[...], deep.astype(F32))
    deep_out[...], depth_out[...], diag_out[...] = fields[3], fields[1], fields[2]
    to_right, to_left = right[...], left[...]
    lane = iota((ROWS, 128), 1)
    to_right = jnp.where((lane >= 3 * LEV) & (lane < 4 * LEV), pltpu.roll(to_right, LEV, 1), to_right)
    for i, field in enumerate(fields):
        tile = field[:, COLS - 128:]
        tile = pltpu.roll(tile, 128 - 2 * i, 1) if i else tile
        to_right = jnp.where((lane >= 126 - 2 * i) & (lane < 128 - 2 * i), tile, to_right)
        tile = field[:, :128]
        tile = pltpu.roll(tile, 3 * i, 1) if i else tile
        to_left = jnp.where((lane >= 3 * i) & (lane < 3 * i + 3), tile, to_left)
    rows_0 = edge_rows[0:SLOT] - 0.5 * edge_rows[SLOT:2 * SLOT]
    rows_1 = edge_rows[2 * SLOT:3 * SLOT] - 0.5 * edge_rows[3 * SLOT:4 * SLOT]
    rows_2 = edge_rows[4 * SLOT:5 * SLOT]
    lane = iota((SLOT, 128), 1)
    corner_right = corner_left = jnp.zeros((SLOT, 128), F32)
    for i, rows in enumerate((rows_0, rows_1, rows_2)):
        tile = rows[:, COLS - 128:]
        tile = pltpu.roll(tile, 128 - 2 * i, 1) if i else tile
        corner_right = jnp.where((lane >= 126 - 2 * i) & (lane < 128 - 2 * i), tile, corner_right)
        tile = rows[:, :128]
        tile = pltpu.roll(tile, 3 * i, 1) if i else tile
        corner_left = jnp.where((lane >= 3 * i) & (lane < 3 * i + 3), tile, corner_left)
    even = lax.axis_index("bx") % 2 == 0
    first_out[:ROWS] = jnp.where(even, to_right, to_left)
    second_out[:ROWS] = jnp.where(even, to_left, to_right)
    first_out[ROWS:] = jnp.where(even, corner_right, corner_left)
    second_out[ROWS:] = jnp.where(even, corner_left, corner_right)


def lane_tile(from_right, from_left, i):
    lane = iota(from_right.shape, 1)
    if i:
        from_right, from_left = pltpu.roll(from_right, 128 - 3 * i, 1), pltpu.roll(from_left, 2 * i, 1)
    return jnp.where(lane < 3, from_right, jnp.where(lane >= 126, from_left, 0.0))


def columns_kernel(weights, first, second, first_in, second_in, forcing, deep_in, depth_in, diag, edge_rows, after,
                   first_out, second_out, forcing_wide, depth_wide, diag_wide, flux_left, flux_right):
    own_right, own_left = by_side("bx", first[...], second[...])
    from_right, from_left = by_side("bx", first_in[...], second_in[...])
    deep_f, depth = deep_in[...], depth_in[...]
    lane = iota((ROWS, 128), 1)
    at = iota((8, 128), 1)
    mix, weight = weights[0:1, :128], weights[8:9, :128]
    of_lane = jnp.where(at < LEV, at, jnp.where(at < 2 * LEV, at - LEV, 100))[:1].astype(F32)

    def face(west, east, flow, west_deep, east_deep):
        flux = 0.5 * flow * (west + east) - mix * (east - west)
        flux = jnp.where(of_lane < jnp.minimum(west_deep, east_deep), flux, 0.0)
        return flux, jnp.sum(flux * weight, axis=1, keepdims=True)

    own, seen = own_left[:ROWS], from_left[:ROWS]
    flux, west_sum = face(seen, pltpu.roll(own, 64, 1), pltpu.roll(seen, 128 - 2 * LEV, 1), seen[:, 121:122], deep_f[:, :1])
    flux_left[...] = flux
    own, seen = own_right[:ROWS], from_right[:ROWS]
    flux, east_sum = face(own, pltpu.roll(seen, 64, 1), pltpu.roll(own, 128 - 2 * LEV, 1), deep_f[:, COLS - 1:], seen[:, 9:10])
    flux_right[...] = flux

    mine = forcing[...]
    tiles = (
        mine[:, :128] + jnp.where(lane == 0, west_sum, 0.0),
        mine[:, 128:] - jnp.where(lane == 127, east_sum, 0.0),
        lane_tile(from_right[:ROWS], from_left[:ROWS], 0)
        + jnp.where(lane == 0, east_sum, jnp.where(lane == 127, -west_sum, 0.0)),
    )
    wide = jnp.concatenate(tiles, axis=1)
    forcing_wide[...] = wide
    depth_w = jnp.concatenate([depth, lane_tile(from_right[:ROWS], from_left[:ROWS], 1)], axis=1)
    diag_w = jnp.concatenate([diag[...], lane_tile(from_right[:ROWS], from_left[:ROWS], 2)], axis=1)
    deep_w = jnp.concatenate([deep_f, lane_tile(from_right[:ROWS], from_left[:ROWS], 3)], axis=1)
    depth_wide[...] = depth_w
    diag_wide[...] = diag_w

    def rows(value, i):
        return jnp.concatenate([value, lane_tile(from_right[ROWS:], from_left[ROWS:], i)], axis=1)

    nothing = jnp.zeros((SLOT, 128), F32)
    two_0, two_1 = edge_rows[SLOT:2 * SLOT], edge_rows[3 * SLOT:4 * SLOT]
    both_0 = rows(edge_rows[0:SLOT] - 0.5 * two_0, 0)
    both_1 = rows(edge_rows[2 * SLOT:3 * SLOT] - 0.5 * two_1, 1)
    north_1 = rows(edge_rows[4 * SLOT:5 * SLOT], 2)
    even = lax.axis_index("by") % 2 == 0
    up = (both_1, jnp.concatenate([two_1, nothing], axis=1), north_1, jnp.concatenate(
        [wide[62:64], deep_w[63:64], depth_w[62:64], diag_w[63:64], jnp.zeros((2, WIDE), F32)], axis=0))
    down = (both_0, jnp.concatenate([two_0, nothing], axis=1), jnp.zeros((SLOT, WIDE), F32), jnp.concatenate(
        [wide[0:3], deep_w[0:1], depth_w[0:2], diag_w[0:2]], axis=0))
    for i in range(4):
        place = slice(i * SLOT, i * SLOT + (SLOT if i < 3 else 8))
        first_out[place] = jnp.where(even, up[i], down[i])
        second_out[place] = jnp.where(even, down[i], up[i])


def operate(field, half_depth, diag):
    east = pltpu.roll(field, WIDE - 1, 1)
    north = pltpu.roll(field, TALL - 1, 0)
    corner = pltpu.roll(north, WIDE - 1, 1)
    plus = half_depth * (corner - field)
    minus = half_depth * (east - north)
    return (diag * field - plus + pltpu.roll(minus, 1, 1)
            + pltpu.roll(pltpu.roll(plus, 1, 1) - minus, 1, 0)), plus, minus


def solver_kernel(weights, first, second, first_in, second_in, forcing, depth, diag, after,
                  zero_out, one_out, two_out, sums_out, flux_rows):
    own_up, own_down = by_side("by", first[...], second[...])
    above, beneath = by_side("by", first_in[...], second_in[...])
    level = iota((SLOT, WIDE), 0)
    mix, weight = (jnp.concatenate([weights[i:i + SLOT], weights[i:i + SLOT, :128]], axis=1) for i in (16, 16 + SLOT))
    level_f = level.astype(F32)

    def face(south, north, south_deep, north_deep):
        flow = south[2 * SLOT:3 * SLOT]
        wet = level_f < jnp.minimum(south_deep, north_deep)

        def flux(low, high):
            columns = low.shape[1]
            value = 0.5 * flow[:, :columns] * (low + high) - mix[:, :columns] * (high - low)
            return jnp.where(wet[:, :columns], value, 0.0)

        both = flux(south[:SLOT], north[:SLOT])
        two = flux(south[SLOT:2 * SLOT, :COLS], north[SLOT:2 * SLOT, :COLS])
        return jnp.sum(both * weight, axis=0, keepdims=True), both[:, :COLS] + 0.5 * two, two

    top, top_one, top_two = face(own_up, above, own_up[74:75], above[75:76])
    bottom, bottom_one, bottom_two = face(beneath, own_down, beneath[74:75], own_down[75:76])

    for i, flux in enumerate((bottom_one, bottom_two, top_one, top_two)):
        flux_rows[i * SLOT:(i + 1) * SLOT] = flux

    def blank(count):
        return jnp.zeros((count, WIDE), F32)

    own_row = iota((ROWS, WIDE), 0)
    mine = forcing[...] + jnp.where(own_row == 0, bottom, jnp.where(own_row == ROWS - 1, -top, 0.0))
    field = jnp.concatenate([
        jnp.concatenate([blank(6), beneath[72:73], beneath[73:74] - bottom], axis=0), mine,
        jnp.concatenate([above[72:73] + top, above[73:75], blank(5)], axis=0)], axis=0)
    half_depth = 0.5 * jnp.concatenate([
        jnp.concatenate([blank(6), beneath[75:77]], axis=0), depth[...],
        jnp.concatenate([above[76:78], blank(6)], axis=0)], axis=0)
    diag_all = jnp.concatenate([
        jnp.concatenate([blank(7), beneath[77:78]], axis=0), diag[...],
        jnp.concatenate([above[78:80], blank(6)], axis=0)], axis=0)
    last = lax.axis_index("by") == lax.axis_size("by") - 1
    inside = iota((TALL, WIDE), 0) < jnp.where(last, ROWS + 8, TALL)

    image, _, _ = operate(field, half_depth, diag_all)
    image = jnp.where(inside, image, 0.0)
    twice, _, _ = operate(image, half_depth, diag_all)
    twice = jnp.where(inside, twice, 0.0)
    _, plus, minus = operate(twice, half_depth, diag_all)
    east = pltpu.roll(twice, WIDE - 1, 1)
    north = pltpu.roll(twice, TALL - 1, 0)
    corner = pltpu.roll(north, WIDE - 1, 1)
    energy = diag_all * twice * twice + plus * (corner - twice) + minus * (east - north)

    def own(value):
        return value[8:8 + ROWS, :COLS]

    v_0, v_1, v_2 = own(field), own(image), own(twice)
    zero_out[...], one_out[...], two_out[...] = v_0, v_1, v_2
    lane = iota((128, 128), 1)
    sums = jnp.zeros((128, 128), F32)
    for i, product in enumerate((v_0 * v_0, v_0 * v_1, v_1 * v_1, v_1 * v_2, v_2 * v_2, own(energy))):
        sums = jnp.where(lane == i, jnp.sum(product, keepdims=True), sums)
    sums_out[...] = sums


def surface_kernel(sums, zero, one, two, flux_rows, new_one, new_two, inner_one, inner_two,
                   surface_out, full_one, full_two, surface, strips, sems):
    row = iota((8, COLS), 0)
    stores = []
    for i, (source, target) in enumerate(((new_one, full_one), (new_two, full_two))):
        part = pl.ds(ROWS - CHUNK, CHUNK - 8)
        stores.append(pltpu.make_async_copy(source.at[:, part], target.at[:, part], sems.at[4 + i]))
        stores[-1].start()
    for i, (source, at, sign, target) in enumerate((
            (new_one, 0, 1.0, full_one), (new_two, 0, 1.0, full_two),
            (new_one, 7, -1.0, full_one), (new_two, 7, -1.0, full_two))):
        start = 0 if at == 0 else ROWS - 8
        for k in range(LEV):
            place = i * SLOT + k
            strips[i, k] = source[k, start:start + 8] + jnp.where(row == at, sign * flux_rows[place:place + 1], 0.0)
        stores.append(pltpu.make_async_copy(strips.at[i], target.at[:, pl.ds(start, 8)], sems.at[i]))
        stores[-1].start()
    total = jnp.sum(sums[...], axis=0, keepdims=True)
    m = [total[:, i:i + 1] for i in range(6)]
    a_0 = m[0] / m[1]
    rr_1 = m[0] - 2.0 * a_0 * m[1] + a_0 * a_0 * m[2]
    rar_1 = m[1] - 2.0 * a_0 * m[2] + a_0 * a_0 * m[3]
    b_1 = rr_1 / m[0]
    a_1 = rr_1 / (rar_1 - b_1 * rr_1 / a_0)
    grow = 1.0 + b_1
    p_1 = -(a_0 + a_1 * grow)
    p_2 = a_1 * a_0
    rr_2 = m[0] + p_1 * p_1 * m[2] + p_2 * p_2 * m[4] + 2.0 * (p_1 * m[1] + p_2 * m[2] + p_1 * p_2 * m[3])
    rar_2 = m[1] + p_1 * p_1 * m[3] + p_2 * p_2 * m[5] + 2.0 * (p_1 * m[2] + p_2 * m[3] + p_1 * p_2 * m[4])
    b_2 = rr_2 / rr_1
    a_2 = rr_2 / (rar_2 - b_2 * rr_2 / a_1)
    w_0 = a_0 + a_1 * grow + a_2 * (1.0 + b_2 * grow)
    w_1 = -a_1 * a_0 + a_2 * (p_1 - b_2 * a_0)
    w_2 = a_2 * p_2
    surface[...] = w_0 * zero[...] + w_1 * one[...] + w_2 * two[...]
    stores.append(pltpu.make_async_copy(surface, surface_out, sems.at[6]))
    stores[-1].start()
    wait_all(stores)


def tracers_kernel(weights, one, two, east, north, deep_in, part_one, part_two, east_deep, north_deep, edge):
    deep = deep_in[...].astype(jnp.int32)
    at_row, at_col = iota((ROWS, COLS), 0), iota((ROWS, COLS), 1)
    east_deep[...] = jnp.where(at_col < COLS - 1, jnp.minimum(deep, pltpu.roll(deep, COLS - 1, 1)), 0)
    north_deep[...] = jnp.where(at_row < ROWS - 1, jnp.minimum(deep, pltpu.roll(deep, ROWS - 1, 0)), 0)
    edge[...] = jnp.zeros(edge.shape, F32)
    row = iota((CHUNK, COLS), 0)

    @pl.loop(0, ROWS // CHUNK)
    def _(chunk):
        start = pl.multiple_of(chunk * CHUNK, CHUNK)
        part = pl.ds(start, CHUNK)
        here, to_east, to_north = deep_in[part].astype(jnp.int32), east_deep[part], north_deep[part]

        def level(k, falls):
            flow_e, flow_n = east[k, part].astype(F32), north[k, part].astype(F32)
            mix = 2.0 * weights[pl.ds(16 + k, 1)]
            below = jnp.minimum(k + 1, LEV - 1)
            wet, wet_east, wet_north = here > k, to_east > k, to_north > k
            east_own, east_next = jnp.where(wet_east, flow_e + mix, 0.0), jnp.where(wet_east, flow_e - mix, 0.0)
            north_own, north_next = jnp.where(wet_north, flow_n + mix, 0.0), jnp.where(wet_north, flow_n - mix, 0.0)
            fall_w = jnp.where(here > k + 1, weights[pl.ds(16 + 2 * SLOT + k, 1)], 0.0)
            kept_falls = []
            for i, (source, target) in enumerate(((one, part_one), (two, part_two))):
                c = source[k, part]
                e = east_own * c + east_next * pltpu.roll(c, COLS - 1, 1)
                nxt = jnp.where(row == CHUNK - 1, source[k, pl.ds(start + CHUNK, 1)], pltpu.roll(c, CHUNK - 1, 0))
                n = north_own * c + north_next * nxt
                place = pl.ds(i * SLOT + k, 1)
                n_south = jnp.where(row == 0, edge[place], pltpu.roll(n, 1, 0))
                edge[place] = n[CHUNK - 1:]
                fall = fall_w * (source[below, part] - c)
                target[k, part] = jnp.where(
                    wet, c + (fall - falls[i]) - 0.5 * ((e - pltpu.roll(e, 1, 1)) + (n - n_south)), 0.0)
                kept_falls.append(fall)
            return tuple(kept_falls)

        nothing = jnp.zeros((CHUNK, COLS), F32)
        lax.fori_loop(0, LEV, level, (nothing, nothing), unroll=TRACERS_UNROLL)


def edges_kernel(flux_left, flux_right, part_one, part_two, one_out, two_out, new_one, new_two, sems):
    kept = ((8, CHUNK - 8), (CHUNK, CHUNK), (2 * CHUNK, CHUNK))
    stores = []
    lane = iota((CHUNK, 128), 1)
    for chunk in range(ROWS // CHUNK):
        part = pl.ds(chunk * CHUNK, CHUNK)
        west_flux, east_flux = flux_left[part], flux_right[part]
        for i, (source, target, out) in enumerate(((part_one, new_one, one_out), (part_two, new_two, two_out))):
            for k in range(LEV):
                at = k + i * LEV
                seam = pltpu.roll(west_flux, 128 - at, 1) if at else west_flux
                target[k, part, :128] = source[k, part, :128] + jnp.where(lane == 0, seam, 0.0)
                seam = pltpu.roll(east_flux, 127 - at, 1)
                target[k, part, 128:] = source[k, part, 128:] - jnp.where(lane == 127, seam, 0.0)
            if chunk < len(kept):
                place = pl.ds(*kept[chunk])
                stores.append(pltpu.make_async_copy(target.at[:, place], out.at[:, place], sems.at[i, chunk]))
                stores[-1].start()
    wait_all(stores)


def cost(flops, moved):
    return pl.CostEstimate(flops=flops, bytes_accessed=moved, transcendentals=0)


def on_device(*arrays):
    (tracer_one, tracer_two, east_flow, north_flow, depth_levels, side_mix, vert_mix, thickness,
     corner_depth, diagonal) = (pltpu.with_memory_space_constraint(array, pltpu.HBM) for array in arrays)
    n_by, n_bx = lax.axis_size("by"), lax.axis_size("bx")
    cells = LEV * ROWS * COLS
    plane, wide, tile = shape(ROWS, COLS), shape(ROWS, WIDE), shape(ROWS, 128)
    block, taller = shape(LEV, ROWS, COLS), shape(LEV, ROWS + 8, COLS)
    half = jax.ShapeDtypeStruct((LEV, ROWS, COLS), jnp.bfloat16)
    column_message, row_message = shape(ROWS + SLOT, 128), shape(3 * SLOT + 8, WIDE)
    flat, flat_int = pltpu.VMEM((ROWS, COLS), F32), pltpu.VMEM((ROWS, COLS), jnp.int32)
    level_list = pltpu.SMEM((LEV,), F32)
    transfers = pltpu.SemaphoreType.DMA((4, ROWS // CHUNK))
    first, second, forcing, deep, depth, diag, edge_rows, weights, one, two, east, north = pl.pallas_call(
        forcing_kernel,
        out_shape=(column_message, column_message, plane, plane, plane, plane, shape(5 * SLOT, COLS),
                   shape(16 + 3 * SLOT, COLS), taller, taller, half, half),
        in_specs=[HBM] * 10,
        out_specs=(VMEM,) * 12,
        scratch_shapes=[level_list] * 3 + [flat_int, flat, flat] + [flat_int] * 2 + [flat] * 3
        + [pltpu.VMEM((ROWS, 128), F32)] * 2 + [transfers, pltpu.SemaphoreType.DMA((6,))],
        compiler_params=PARAMS, cost_estimate=cost(30 * cells, 12 * cells), name="forcing",
    )(side_mix, vert_mix, thickness, tracer_one, tracer_two, east_flow, north_flow, depth_levels, corner_depth, diagonal)
    part_one, part_two = pl.pallas_call(
        tracers_kernel,
        out_shape=(block, block),
        in_specs=[VMEM] * 6,
        out_specs=(VMEM,) * 2,
        scratch_shapes=[flat_int] * 2 + [pltpu.VMEM((2 * SLOT, COLS), F32)],
        compiler_params=PARAMS, cost_estimate=cost(60 * cells, 20 * cells), name="tracers",
    )(weights, one, two, east, north, deep)
    first_in, second_in = swap_both(first, second, "bx", n_bx, True)
    row_first, row_second, forcing, depth, diag, flux_left, flux_right = pl.pallas_call(
        columns_kernel,
        out_shape=(row_message, row_message, wide, wide, wide, tile, tile),
        in_specs=[VMEM] * 10 + [HBM],
        out_specs=(VMEM,) * 7,
        compiler_params=PARAMS, cost_estimate=cost(10**6, 10**6), name="columns",
    )(weights, first, second, first_in, second_in, forcing, deep, depth, diag, edge_rows, part_one)
    row_first_in, row_second_in = swap_both(row_first, row_second, "by", n_by, False)
    inner_one, inner_two, edge_one, edge_two = pl.pallas_call(
        edges_kernel,
        out_shape=(block, block, block, block),
        in_specs=[VMEM] * 4,
        out_specs=(HBM,) * 2 + (VMEM,) * 2,
        scratch_shapes=[pltpu.SemaphoreType.DMA((2, ROWS // CHUNK))],
        compiler_params=PARAMS, cost_estimate=cost(10 * cells, 10 * cells), name="edges",
    )(flux_left, flux_right, part_one, part_two)
    v_0, v_1, v_2, sums, flux_rows = pl.pallas_call(
        solver_kernel,
        out_shape=(plane, plane, plane, shape(128, 128), shape(4 * SLOT, COLS)),
        in_specs=[VMEM] * 8 + [HBM],
        out_specs=(VMEM,) * 5,
        compiler_params=PARAMS, cost_estimate=cost(4 * 10**6, 10**6), name="solver",
    )(weights, row_first, row_second, row_first_in, row_second_in, forcing, depth, diag, edge_one)
    sums = lax.all_to_all(sums[:n_by * n_bx], ("by", "bx"), 0, 0, tiled=True)
    surface, new_one, new_two = pl.pallas_call(
        surface_kernel,
        out_shape=(plane, block, block),
        in_specs=[VMEM] * 7 + [HBM] * 2,
        out_specs=(HBM,) * 3,
        input_output_aliases={7: 1, 8: 2},
        scratch_shapes=[flat, pltpu.VMEM((4, LEV, 8, COLS), F32), pltpu.SemaphoreType.DMA((7,))],
        compiler_params=PARAMS, cost_estimate=cost(10**5, 10**5), name="surface",
    )(sums, v_0, v_1, v_2, flux_rows, edge_one, edge_two, inner_one, inner_two)
    return new_one, new_two, surface


def solution(mesh):
    block, field = P(None, "by", "bx"), P("by", "bx")
    return jax.shard_map(
        on_device, mesh=mesh,
        in_specs=(block, block, block, block, field, P(), P(), P(), field, field),
        out_specs=(block, block, field), check_vma=False,
    )
```

```python
import jax
import jax.numpy as jnp
from jax import lax
from jax.experimental import pallas as pl
from jax.experimental.pallas import tpu as pltpu
from jax.sharding import PartitionSpec as P

LEV = 18
CHUNK = 16
SLOT = LEV
BASE = 3 * SLOT
ROWS, COLS = 64, 256
WIDE = COLS + 128
TALL = ROWS + 16
FORCING_UNROLL = 18
TRACERS_UNROLL = 6
F32 = jnp.float32
VMEM = pl.BlockSpec(memory_space=pltpu.VMEM)
SMEM = pl.BlockSpec(memory_space=pltpu.SMEM)
HBM = pl.BlockSpec(memory_space=pl.ANY)
PARAMS = pltpu.CompilerParams(vmem_limit_bytes=16 * 1024 * 1024)


def iota(shape, axis):
    return lax.broadcasted_iota(jnp.int32, shape, axis)


def shape(*dims):
    return jax.ShapeDtypeStruct(dims, F32)


def pairs(size, odd, wrap):
    swaps = []
    for low in range(1 if odd else 0, size, 2):
        high = low + 1
        if high == size and not wrap:
            continue
        swaps += [(low, high % size), (high % size, low)]
    return swaps


def swap_both(first, second, axis, size, wrap):
    return (
        lax.ppermute(first, axis, pairs(size, False, wrap)),
        lax.ppermute(second, axis, pairs(size, True, wrap)),
    )


def by_side(axis, first, second):
    even = lax.axis_index(axis) % 2 == 0
    return jnp.where(even, first, second), jnp.where(even, second, first)


def load_chunks(sources, targets, sems):
    def copy(array, chunk):
        part = pl.ds(pl.multiple_of(chunk * CHUNK, CHUNK), CHUNK)
        return pltpu.make_async_copy(sources[array].at[:, part], targets[array].at[:, part], sems.at[array, chunk])

    return copy


def start_all(copies):
    for copy in copies:
        copy.start()


def wait_all(copies):
    for copy in copies:
        copy.wait()


def forcing_kernel(side_hbm, vert_hbm, thick_hbm, one_hbm, two_hbm, east_hbm, north_hbm, levels_hbm, corner_hbm, diag_hbm,
                   first_out, second_out, forcing_out, deep_out, depth_out, diag_out, edge_rows, weights,
                   one, two, east, north, side, vert, thick, levels, corner, diag, east_deep, north_deep, east_sum, north_sum, column, right, left, sems, small):
    copy = load_chunks((one_hbm, two_hbm, east_hbm, north_hbm), (one, two, east, north), sems)
    chunks = ROWS // CHUNK
    pairs_of = ((levels_hbm, levels), (side_hbm, side), (vert_hbm, vert), (thick_hbm, thick), (corner_hbm, corner), (diag_hbm, diag))
    singles = [pltpu.make_async_copy(a, b, small.at[i]) for i, (a, b) in enumerate(pairs_of)]
    start_all(singles[:4])
    for chunk in range(chunks):
        start_all(copy(array, chunk) for array in range(4))
    start_all(singles[4:])
    for array in (one, two):
        array[:, ROWS:] = jnp.zeros((LEV, 8, COLS), F32)
    wait_all(singles[:4])
    deep = levels[...]
    at_row, at_col = iota((ROWS, COLS), 0), iota((ROWS, COLS), 1)
    east_deep[...] = jnp.where(at_col < COLS - 1, jnp.minimum(deep, pltpu.roll(deep, COLS - 1, 1)), 0)
    north_deep[...] = jnp.where(at_row < ROWS - 1, jnp.minimum(deep, pltpu.roll(deep, ROWS - 1, 0)), 0)
    edge_rows[...] = jnp.zeros(edge_rows.shape, F32)
    row, lane = iota((CHUNK, COLS), 0), iota((CHUNK, 128), 1)
    wait_all(copy(array, 0) for array in range(4))

    @pl.loop(0, chunks)
    def _(chunk):
        @pl.when(chunk + 1 < chunks)
        def _():
            wait_all(copy(array, chunk + 1) for array in range(4))

        start = pl.multiple_of(chunk * CHUNK, CHUNK)
        part = pl.ds(start, CHUNK)
        here, to_east, to_north = levels[part], east_deep[part], north_deep[part]

        def level(k, carry):
            e_sum, n_sum, total, to_right, to_left = carry
            c_one, c_two = one[k, part], two[k, part]
            flow_e, flow_n = east[k, part].astype(F32), north[k, part].astype(F32)
            both = c_one - 0.5 * c_two
            beyond = one[k, pl.ds(start + CHUNK, 1)] - 0.5 * two[k, pl.ds(start + CHUNK, 1)]
            weight, mix = thick[k], 2.0 * side[k]
            below, above = jnp.minimum(k + 1, LEV - 1), jnp.maximum(k - 1, 0)
            fall = (weight - thick[below]) * vert[k]
            fall_above = (thick[above] - weight) * vert[above]
            total = total + both * jnp.where(
                here > k + 1, weight + fall_above - fall, jnp.where(here > k, weight + fall_above, 0.0))
            both, beyond = (0.5 * weight) * both, (0.5 * weight) * beyond
            nxt = pltpu.roll(both, COLS - 1, 1)
            e_sum = e_sum + jnp.where(to_east > k, flow_e * (both + nxt) - mix * (nxt - both), 0.0)
            nxt = jnp.where(row == CHUNK - 1, beyond, pltpu.roll(both, CHUNK - 1, 0))
            n_sum = n_sum + jnp.where(to_north > k, flow_n * (both + nxt) - mix * (nxt - both), 0.0)
            for i, value in enumerate((c_one, c_two, flow_e)):
                at = k + i * LEV
                to_right = jnp.where(lane == at, pltpu.roll(value[:, COLS - 128:], at + 1, 1), to_right)
            for i, value in enumerate((c_one, c_two)):
                at = k + i * LEV + 64
                to_left = jnp.where(lane == at, pltpu.roll(value[:, :128], at, 1), to_left)
            return e_sum, n_sum, total, to_right, to_left

        flat, tile = jnp.zeros((CHUNK, COLS), F32), jnp.zeros((CHUNK, 128), F32)
        result = lax.fori_loop(0, LEV, level, (flat, flat, flat, tile, tile), unroll=FORCING_UNROLL)
        for target, value in zip((east_sum, north_sum, column, right, left), result):
            target[part] = value

    for k in range(LEV):
        rows = (one[k, 0:1], two[k, 0:1], one[k, ROWS - 1:ROWS], two[k, ROWS - 1:ROWS],
                north[k, ROWS - 16:ROWS].astype(F32)[15:])
        for i, value in enumerate(rows):
            edge_rows[i * SLOT + k:i * SLOT + k + 1] = value

    at, level = iota((8, COLS), 1), iota((SLOT, COLS), 0)
    lane_mix = lane_weight = jnp.zeros((8, COLS), F32)
    row_mix = row_weight = row_vert = jnp.zeros((SLOT, COLS), F32)
    for k in range(LEV):
        lane_mix = jnp.where((at == k) | (at == k + LEV), side[k], lane_mix)
        lane_weight = jnp.where(at == k, thick[k], jnp.where(at == k + LEV, -0.5 * thick[k], lane_weight))
        row_mix = jnp.where(level == k, side[k], row_mix)
        row_weight = jnp.where(level == k, thick[k], row_weight)
        row_vert = jnp.where(level == k, vert[k], row_vert)
    weights[...] = jnp.concatenate([lane_mix, lane_weight, row_mix, row_weight, row_vert], axis=0)
    e_sum, n_sum = east_sum[...], north_sum[...]
    forcing = column[...] - (e_sum - pltpu.roll(e_sum, 1, 1)) - (n_sum - pltpu.roll(n_sum, 1, 0))
    forcing_out[...] = forcing
    wait_all(singles[4:])
    depth = jnp.where(deep > 0, corner[...], 0.0)
    fields = (forcing, depth, diag[...], deep.astype(F32))
    deep_out[...], depth_out[...], diag_out[...] = fields[3], fields[1], fields[2]
    to_right, to_left = right[...], left[...]
    lane = iota((ROWS, 128), 1)
    to_right = jnp.where((lane >= 3 * LEV) & (lane < 4 * LEV), pltpu.roll(to_right, LEV, 1), to_right)
    for i, field in enumerate(fields):
        tile = field[:, COLS - 128:]
        tile = pltpu.roll(tile, 128 - 2 * i, 1) if i else tile
        to_right = jnp.where((lane >= 126 - 2 * i) & (lane < 128 - 2 * i), tile, to_right)
        tile = field[:, :128]
        tile = pltpu.roll(tile, 3 * i, 1) if i else tile
        to_left = jnp.where((lane >= 3 * i) & (lane < 3 * i + 3), tile, to_left)
    rows_0 = edge_rows[0:SLOT] - 0.5 * edge_rows[SLOT:2 * SLOT]
    rows_1 = edge_rows[2 * SLOT:3 * SLOT] - 0.5 * edge_rows[3 * SLOT:4 * SLOT]
    rows_2 = edge_rows[4 * SLOT:5 * SLOT]
    lane = iota((SLOT, 128), 1)
    corner_right = corner_left = jnp.zeros((SLOT, 128), F32)
    for i, rows in enumerate((rows_0, rows_1, rows_2)):
        tile = rows[:, COLS - 128:]
        tile = pltpu.roll(tile, 128 - 2 * i, 1) if i else tile
        corner_right = jnp.where((lane >= 126 - 2 * i) & (lane < 128 - 2 * i), tile, corner_right)
        tile = rows[:, :128]
        tile = pltpu.roll(tile, 3 * i, 1) if i else tile
        corner_left = jnp.where((lane >= 3 * i) & (lane < 3 * i + 3), tile, corner_left)
    even = lax.axis_index("bx") % 2 == 0
    first_out[:ROWS] = jnp.where(even, to_right, to_left)
    second_out[:ROWS] = jnp.where(even, to_left, to_right)
    first_out[ROWS:] = jnp.where(even, corner_right, corner_left)
    second_out[ROWS:] = jnp.where(even, corner_left, corner_right)


def lane_tile(from_right, from_left, i):
    lane = iota(from_right.shape, 1)
    if i:
        from_right, from_left = pltpu.roll(from_right, 128 - 3 * i, 1), pltpu.roll(from_left, 2 * i, 1)
    return jnp.where(lane < 3, from_right, jnp.where(lane >= 126, from_left, 0.0))


def columns_kernel(weights, first, second, first_in, second_in, forcing, deep_in, depth_in, diag, edge_rows, after,
                   first_out, second_out, forcing_wide, depth_wide, diag_wide, flux_left, flux_right):
    own_right, own_left = by_side("bx", first[...], second[...])
    from_right, from_left = by_side("bx", first_in[...], second_in[...])
    deep_f, depth = deep_in[...], depth_in[...]
    lane = iota((ROWS, 128), 1)
    at = iota((8, 128), 1)
    mix, weight = weights[0:1, :128], weights[8:9, :128]
    of_lane = jnp.where(at < LEV, at, jnp.where(at < 2 * LEV, at - LEV, 100))[:1].astype(F32)

    def face(west, east, flow, west_deep, east_deep):
        flux = 0.5 * flow * (west + east) - mix * (east - west)
        flux = jnp.where(of_lane < jnp.minimum(west_deep, east_deep), flux, 0.0)
        return flux, jnp.sum(flux * weight, axis=1, keepdims=True)

    own, seen = own_left[:ROWS], from_left[:ROWS]
    flux, west_sum = face(seen, pltpu.roll(own, 64, 1), pltpu.roll(seen, 128 - 2 * LEV, 1), seen[:, 121:122], deep_f[:, :1])
    flux_left[...] = flux
    own, seen = own_right[:ROWS], from_right[:ROWS]
    flux, east_sum = face(own, pltpu.roll(seen, 64, 1), pltpu.roll(own, 128 - 2 * LEV, 1), deep_f[:, COLS - 1:], seen[:, 9:10])
    flux_right[...] = flux

    mine = forcing[...]
    tiles = (
        mine[:, :128] + jnp.where(lane == 0, west_sum, 0.0),
        mine[:, 128:] - jnp.where(lane == 127, east_sum, 0.0),
        lane_tile(from_right[:ROWS], from_left[:ROWS], 0)
        + jnp.where(lane == 0, east_sum, jnp.where(lane == 127, -west_sum, 0.0)),
    )
    wide = jnp.concatenate(tiles, axis=1)
    forcing_wide[...] = wide
    depth_w = jnp.concatenate([depth, lane_tile(from_right[:ROWS], from_left[:ROWS], 1)], axis=1)
    diag_w = jnp.concatenate([diag[...], lane_tile(from_right[:ROWS], from_left[:ROWS], 2)], axis=1)
    deep_w = jnp.concatenate([deep_f, lane_tile(from_right[:ROWS], from_left[:ROWS], 3)], axis=1)
    depth_wide[...] = depth_w
    diag_wide[...] = diag_w

    def rows(value, i):
        return jnp.concatenate([value, lane_tile(from_right[ROWS:], from_left[ROWS:], i)], axis=1)

    nothing = jnp.zeros((SLOT, 128), F32)
    two_0, two_1 = edge_rows[SLOT:2 * SLOT], edge_rows[3 * SLOT:4 * SLOT]
    both_0 = rows(edge_rows[0:SLOT] - 0.5 * two_0, 0)
    both_1 = rows(edge_rows[2 * SLOT:3 * SLOT] - 0.5 * two_1, 1)
    north_1 = rows(edge_rows[4 * SLOT:5 * SLOT], 2)
    even = lax.axis_index("by") % 2 == 0
    up = (both_1, jnp.concatenate([two_1, nothing], axis=1), north_1, jnp.concatenate(
        [wide[62:64], deep_w[63:64], depth_w[62:64], diag_w[63:64], jnp.zeros((2, WIDE), F32)], axis=0))
    down = (both_0, jnp.concatenate([two_0, nothing], axis=1), jnp.zeros((SLOT, WIDE), F32), jnp.concatenate(
        [wide[0:3], deep_w[0:1], depth_w[0:2], diag_w[0:2]], axis=0))
    for i in range(4):
        place = slice(i * SLOT, i * SLOT + (SLOT if i < 3 else 8))
        first_out[place] = jnp.where(even, up[i], down[i])
        second_out[place] = jnp.where(even, down[i], up[i])


def operate(field, half_depth, diag):
    east = pltpu.roll(field, WIDE - 1, 1)
    north = pltpu.roll(field, TALL - 1, 0)
    corner = pltpu.roll(north, WIDE - 1, 1)
    plus = half_depth * (corner - field)
    minus = half_depth * (east - north)
    return (diag * field - plus + pltpu.roll(minus, 1, 1)
            + pltpu.roll(pltpu.roll(plus, 1, 1) - minus, 1, 0)), plus, minus


def solver_kernel(weights, first, second, first_in, second_in, forcing, depth, diag, after,
                  zero_out, one_out, two_out, sums_out, flux_rows):
    own_up, own_down = by_side("by", first[...], second[...])
    above, beneath = by_side("by", first_in[...], second_in[...])
    level = iota((SLOT, WIDE), 0)
    mix, weight = (jnp.concatenate([weights[i:i + SLOT], weights[i:i + SLOT, :128]], axis=1) for i in (16, 16 + SLOT))
    level_f = level.astype(F32)

    def face(south, north, south_deep, north_deep):
        flow = south[2 * SLOT:3 * SLOT]
        wet = level_f < jnp.minimum(south_deep, north_deep)

        def flux(low, high):
            columns = low.shape[1]
            value = 0.5 * flow[:, :columns] * (low + high) - mix[:, :columns] * (high - low)
            return jnp.where(wet[:, :columns], value, 0.0)

        both = flux(south[:SLOT], north[:SLOT])
        two = flux(south[SLOT:2 * SLOT, :COLS], north[SLOT:2 * SLOT, :COLS])
        return jnp.sum(both * weight, axis=0, keepdims=True), both[:, :COLS] + 0.5 * two, two

    top, top_one, top_two = face(own_up, above, own_up[BASE + 2:BASE + 3], above[BASE + 3:BASE + 4])
    bottom, bottom_one, bottom_two = face(beneath, own_down, beneath[BASE + 2:BASE + 3], own_down[BASE + 3:BASE + 4])

    for i, flux in enumerate((bottom_one, bottom_two, top_one, top_two)):
        flux_rows[i * SLOT:(i + 1) * SLOT] = flux

    def blank(count):
        return jnp.zeros((count, WIDE), F32)

    own_row = iota((ROWS, WIDE), 0)
    mine = forcing[...] + jnp.where(own_row == 0, bottom, jnp.where(own_row == ROWS - 1, -top, 0.0))
    field = jnp.concatenate([
        jnp.concatenate([blank(6), beneath[BASE:BASE + 1], beneath[BASE + 1:BASE + 2] - bottom], axis=0), mine,
        jnp.concatenate([above[BASE:BASE + 1] + top, above[BASE + 1:BASE + 3], blank(5)], axis=0)], axis=0)
    half_depth = 0.5 * jnp.concatenate([
        jnp.concatenate([blank(6), beneath[BASE + 3:BASE + 5]], axis=0), depth[...],
        jnp.concatenate([above[BASE + 4:BASE + 6], blank(6)], axis=0)], axis=0)
    diag_all = jnp.concatenate([
        jnp.concatenate([blank(7), beneath[BASE + 5:BASE + 6]], axis=0), diag[...],
        jnp.concatenate([above[BASE + 6:BASE + 8], blank(6)], axis=0)], axis=0)
    last = lax.axis_index("by") == lax.axis_size("by") - 1
    inside = iota((TALL, WIDE), 0) < jnp.where(last, ROWS + 8, TALL)

    image, _, _ = operate(field, half_depth, diag_all)
    image = jnp.where(inside, image, 0.0)
    twice, _, _ = operate(image, half_depth, diag_all)
    twice = jnp.where(inside, twice, 0.0)
    _, plus, minus = operate(twice, half_depth, diag_all)
    east = pltpu.roll(twice, WIDE - 1, 1)
    north = pltpu.roll(twice, TALL - 1, 0)
    corner = pltpu.roll(north, WIDE - 1, 1)
    energy = diag_all * twice * twice + plus * (corner - twice) + minus * (east - north)

    def own(value):
        return value[8:8 + ROWS, :COLS]

    v_0, v_1, v_2 = own(field), own(image), own(twice)
    zero_out[...], one_out[...], two_out[...] = v_0, v_1, v_2
    lane = iota((128, 128), 1)
    sums = jnp.zeros((128, 128), F32)
    for i, product in enumerate((v_0 * v_0, v_0 * v_1, v_1 * v_1, v_1 * v_2, v_2 * v_2, own(energy))):
        sums = jnp.where(lane == i, jnp.sum(product, keepdims=True), sums)
    sums_out[...] = sums


def surface_kernel(sums, zero, one, two, flux_rows, new_one, new_two, inner_one, inner_two,
                   surface_out, full_one, full_two, surface, strips, sems):
    row = iota((8, COLS), 0)
    stores = []
    for i, (source, target) in enumerate(((new_one, full_one), (new_two, full_two))):
        part = pl.ds(ROWS - CHUNK, CHUNK - 8)
        stores.append(pltpu.make_async_copy(source.at[:, part], target.at[:, part], sems.at[4 + i]))
        stores[-1].start()
    for i, (source, at, sign, target) in enumerate((
            (new_one, 0, 1.0, full_one), (new_two, 0, 1.0, full_two),
            (new_one, 7, -1.0, full_one), (new_two, 7, -1.0, full_two))):
        start = 0 if at == 0 else ROWS - 8
        for k in range(LEV):
            place = i * SLOT + k
            strips[i, k] = source[k, start:start + 8] + jnp.where(row == at, sign * flux_rows[place:place + 1], 0.0)
        stores.append(pltpu.make_async_copy(strips.at[i], target.at[:, pl.ds(start, 8)], sems.at[i]))
        stores[-1].start()
    total = jnp.sum(sums[...], axis=0, keepdims=True)
    m = [total[:, i:i + 1] for i in range(6)]
    a_0 = m[0] / m[1]
    rr_1 = m[0] - 2.0 * a_0 * m[1] + a_0 * a_0 * m[2]
    rar_1 = m[1] - 2.0 * a_0 * m[2] + a_0 * a_0 * m[3]
    b_1 = rr_1 / m[0]
    a_1 = rr_1 / (rar_1 - b_1 * rr_1 / a_0)
    grow = 1.0 + b_1
    p_1 = -(a_0 + a_1 * grow)
    p_2 = a_1 * a_0
    rr_2 = m[0] + p_1 * p_1 * m[2] + p_2 * p_2 * m[4] + 2.0 * (p_1 * m[1] + p_2 * m[2] + p_1 * p_2 * m[3])
    rar_2 = m[1] + p_1 * p_1 * m[3] + p_2 * p_2 * m[5] + 2.0 * (p_1 * m[2] + p_2 * m[3] + p_1 * p_2 * m[4])
    b_2 = rr_2 / rr_1
    a_2 = rr_2 / (rar_2 - b_2 * rr_2 / a_1)
    w_0 = a_0 + a_1 * grow + a_2 * (1.0 + b_2 * grow)
    w_1 = -a_1 * a_0 + a_2 * (p_1 - b_2 * a_0)
    w_2 = a_2 * p_2
    surface[...] = w_0 * zero[...] + w_1 * one[...] + w_2 * two[...]
    stores.append(pltpu.make_async_copy(surface, surface_out, sems.at[6]))
    stores[-1].start()
    wait_all(stores)


def tracers_kernel(weights, one, two, east, north, deep_in, part_one, part_two, east_deep, north_deep, edge):
    deep = deep_in[...].astype(jnp.int32)
    at_row, at_col = iota((ROWS, COLS), 0), iota((ROWS, COLS), 1)
    east_deep[...] = jnp.where(at_col < COLS - 1, jnp.minimum(deep, pltpu.roll(deep, COLS - 1, 1)), 0)
    north_deep[...] = jnp.where(at_row < ROWS - 1, jnp.minimum(deep, pltpu.roll(deep, ROWS - 1, 0)), 0)
    edge[...] = jnp.zeros(edge.shape, F32)
    row = iota((CHUNK, COLS), 0)

    @pl.loop(0, ROWS // CHUNK)
    def _(chunk):
        start = pl.multiple_of(chunk * CHUNK, CHUNK)
        part = pl.ds(start, CHUNK)
        here, to_east, to_north = deep_in[part].astype(jnp.int32), east_deep[part], north_deep[part]

        def level(k, falls):
            flow_e, flow_n = east[k, part].astype(F32), north[k, part].astype(F32)
            mix = 2.0 * weights[pl.ds(16 + k, 1)]
            below = jnp.minimum(k + 1, LEV - 1)
            wet, wet_east, wet_north = here > k, to_east > k, to_north > k
            east_own, east_next = jnp.where(wet_east, flow_e + mix, 0.0), jnp.where(wet_east, flow_e - mix, 0.0)
            north_own, north_next = jnp.where(wet_north, flow_n + mix, 0.0), jnp.where(wet_north, flow_n - mix, 0.0)
            fall_w = jnp.where(here > k + 1, weights[pl.ds(16 + 2 * SLOT + k, 1)], 0.0)
            kept_falls = []
            for i, (source, target) in enumerate(((one, part_one), (two, part_two))):
                c = source[k, part]
                e = east_own * c + east_next * pltpu.roll(c, COLS - 1, 1)
                nxt = jnp.where(row == CHUNK - 1, source[k, pl.ds(start + CHUNK, 1)], pltpu.roll(c, CHUNK - 1, 0))
                n = north_own * c + north_next * nxt
                place = pl.ds(i * SLOT + k, 1)
                n_south = jnp.where(row == 0, edge[place], pltpu.roll(n, 1, 0))
                edge[place] = n[CHUNK - 1:]
                fall = fall_w * (source[below, part] - c)
                target[k, part] = jnp.where(
                    wet, c + (fall - falls[i]) - 0.5 * ((e - pltpu.roll(e, 1, 1)) + (n - n_south)), 0.0)
                kept_falls.append(fall)
            return tuple(kept_falls)

        nothing = jnp.zeros((CHUNK, COLS), F32)
        lax.fori_loop(0, LEV, level, (nothing, nothing), unroll=TRACERS_UNROLL)


def edges_kernel(flux_left, flux_right, part_one, part_two, one_out, two_out, new_one, new_two, sems):
    kept = ((8, CHUNK - 8), (CHUNK, CHUNK), (2 * CHUNK, CHUNK))
    stores = []
    lane = iota((CHUNK, 128), 1)
    for chunk in range(ROWS // CHUNK):
        part = pl.ds(chunk * CHUNK, CHUNK)
        west_flux, east_flux = flux_left[part], flux_right[part]
        for i, (source, target, out) in enumerate(((part_one, new_one, one_out), (part_two, new_two, two_out))):
            for k in range(LEV):
                at = k + i * LEV
                seam = pltpu.roll(west_flux, 128 - at, 1) if at else west_flux
                target[k, part, :128] = source[k, part, :128] + jnp.where(lane == 0, seam, 0.0)
                seam = pltpu.roll(east_flux, 127 - at, 1)
                target[k, part, 128:] = source[k, part, 128:] - jnp.where(lane == 127, seam, 0.0)
            if chunk < len(kept):
                place = pl.ds(*kept[chunk])
                stores.append(pltpu.make_async_copy(target.at[:, place], out.at[:, place], sems.at[i, chunk]))
                stores[-1].start()
    wait_all(stores)


def cost(flops, moved):
    return pl.CostEstimate(flops=flops, bytes_accessed=moved, transcendentals=0)


def on_device(*arrays):
    (tracer_one, tracer_two, east_flow, north_flow, depth_levels, side_mix, vert_mix, thickness,
     corner_depth, diagonal) = (pltpu.with_memory_space_constraint(array, pltpu.HBM) for array in arrays)
    n_by, n_bx = lax.axis_size("by"), lax.axis_size("bx")
    cells = LEV * ROWS * COLS
    plane, wide, tile = shape(ROWS, COLS), shape(ROWS, WIDE), shape(ROWS, 128)
    block, taller = shape(LEV, ROWS, COLS), shape(LEV, ROWS + 8, COLS)
    half = jax.ShapeDtypeStruct((LEV, ROWS, COLS), jnp.bfloat16)
    column_message, row_message = shape(ROWS + SLOT, 128), shape(BASE + 8, WIDE)
    flat, flat_int = pltpu.VMEM((ROWS, COLS), F32), pltpu.VMEM((ROWS, COLS), jnp.int32)
    level_list = pltpu.SMEM((LEV,), F32)
    transfers = pltpu.SemaphoreType.DMA((4, ROWS // CHUNK))
    first, second, forcing, deep, depth, diag, edge_rows, weights, one, two, east, north = pl.pallas_call(
        forcing_kernel,
        out_shape=(column_message, column_message, plane, plane, plane, plane, shape(5 * SLOT, COLS),
                   shape(16 + 3 * SLOT, COLS), taller, taller, half, half),
        in_specs=[HBM] * 10,
        out_specs=(VMEM,) * 12,
        scratch_shapes=[level_list] * 3 + [flat_int, flat, flat] + [flat_int] * 2 + [flat] * 3
        + [pltpu.VMEM((ROWS, 128), F32)] * 2 + [transfers, pltpu.SemaphoreType.DMA((6,))],
        compiler_params=PARAMS, cost_estimate=cost(30 * cells, 12 * cells), name="forcing",
    )(side_mix, vert_mix, thickness, tracer_one, tracer_two, east_flow, north_flow, depth_levels, corner_depth, diagonal)
    part_one, part_two = pl.pallas_call(
        tracers_kernel,
        out_shape=(block, block),
        in_specs=[VMEM] * 6,
        out_specs=(VMEM,) * 2,
        scratch_shapes=[flat_int] * 2 + [pltpu.VMEM((2 * SLOT, COLS), F32)],
        compiler_params=PARAMS, cost_estimate=cost(60 * cells, 20 * cells), name="tracers",
    )(weights, one, two, east, north, deep)
    first_in, second_in = swap_both(first, second, "bx", n_bx, True)
    row_first, row_second, forcing, depth, diag, flux_left, flux_right = pl.pallas_call(
        columns_kernel,
        out_shape=(row_message, row_message, wide, wide, wide, tile, tile),
        in_specs=[VMEM] * 10 + [HBM],
        out_specs=(VMEM,) * 7,
        compiler_params=PARAMS, cost_estimate=cost(10**6, 10**6), name="columns",
    )(weights, first, second, first_in, second_in, forcing, deep, depth, diag, edge_rows, part_one)
    row_first_in, row_second_in = swap_both(row_first, row_second, "by", n_by, False)
    inner_one, inner_two, edge_one, edge_two = pl.pallas_call(
        edges_kernel,
        out_shape=(block, block, block, block),
        in_specs=[VMEM] * 4,
        out_specs=(HBM,) * 2 + (VMEM,) * 2,
        scratch_shapes=[pltpu.SemaphoreType.DMA((2, ROWS // CHUNK))],
        compiler_params=PARAMS, cost_estimate=cost(10 * cells, 10 * cells), name="edges",
    )(flux_left, flux_right, part_one, part_two)
    v_0, v_1, v_2, sums, flux_rows = pl.pallas_call(
        solver_kernel,
        out_shape=(plane, plane, plane, shape(128, 128), shape(4 * SLOT, COLS)),
        in_specs=[VMEM] * 8 + [HBM],
        out_specs=(VMEM,) * 5,
        compiler_params=PARAMS, cost_estimate=cost(4 * 10**6, 10**6), name="solver",
    )(weights, row_first, row_second, row_first_in, row_second_in, forcing, depth, diag, edge_one)
    sums = lax.all_to_all(sums[:n_by * n_bx], ("by", "bx"), 0, 0, tiled=True)
    surface, new_one, new_two = pl.pallas_call(
        surface_kernel,
        out_shape=(plane, block, block),
        in_specs=[VMEM] * 7 + [HBM] * 2,
        out_specs=(HBM,) * 3,
        input_output_aliases={7: 1, 8: 2},
        scratch_shapes=[flat, pltpu.VMEM((4, LEV, 8, COLS), F32), pltpu.SemaphoreType.DMA((7,))],
        compiler_params=PARAMS, cost_estimate=cost(10**5, 10**5), name="surface",
    )(sums, v_0, v_1, v_2, flux_rows, edge_one, edge_two, inner_one, inner_two)
    return new_one, new_two, surface


def solution(mesh):
    block, field = P(None, "by", "bx"), P("by", "bx")
    return jax.shard_map(
        on_device, mesh=mesh,
        in_specs=(block, block, block, block, field, P(), P(), P(), field, field),
        out_specs=(block, block, field), check_vma=False,
    )
```
